256 devices in a mesh: chan: 8 (over x, y_lo), row: 32 (over z, y_hi, core).
Axes of the slice: x: 4, y: 4 (y_hi: 2, y_lo: 2; y = y_hi * 2 + y_lo), z: 8, core: 2. Of those that a mesh axis runs over, the one named last changes fastest.
Arguments:
- pair: bfloat16 [2048, 2048, 128], P(('row', 'chan')), may hold values from -6 to 6
- pair_mask: int32 [2048, 2048], P(('row', 'chan')), may hold values 0 or 1
- in_gain: float32 [128], replicated, may hold values from 0.1 to 1.9
- in_bias: float32 [128], replicated, may hold values from -3 to 3
- w_value: bfloat16 [128, 256], replicated, may hold values from -0.5 to 0.5
- w_gate: bfloat16 [128, 256], replicated, may hold values from -0.5 to 0.5
- out_gate_w: bfloat16 [128, 128], replicated, may hold values from -0.5 to 0.5
- out_gain: float32 [128], replicated, may hold values from 0.1 to 1.9
- out_bias: float32 [128], replicated, may hold values from -3 to 3
- w_out: bfloat16 [128, 128], replicated, may hold values from -0.5 to 0.5
Outputs:
- update: bfloat16 [2048, 256, 128], P(('row', 'chan'))
The draws below stay inside these ranges and needn't reach their ends.
All inputs are finite; a program needn't handle non-finite values. No bound on the sum of `pair_mask` on one device may be relied on, other than what follows from the above.
Results may differ from the reference program's by a relative error of at most 0.017.
Values may be sent and summed in bfloat16 or wider, within the bound.
No kernel may reach another device: no remote copies, remote signals or barrier semaphores. Data moves between devices by JAX's collectives and lax.ppermute only.
A program may use at most 128 MiB of HBM per device.

```python
import jax
import jax.numpy as jnp
from jax import lax

CZ = 128
CH = 128
ROW_DEV = 64
N = 2048
WIN = 256
N_CHAN = 8
N_ROW = 32


def touch_ends(values, key, least, largest):
    place = [jax.random.randint(jax.random.fold_in(key, axis), (), 0, length) for axis, length in enumerate(values.shape)]
    main_axis = values.shape.index(max(values.shape))
    neighbour = place[:main_axis] + [(place[main_axis] + 1) % values.shape[main_axis]] + place[main_axis + 1:]
    return values.at[tuple(place)].set(least).at[tuple(neighbour)].set(largest)


def shard_levels(key, extent, shards, low, top_value):
    def one(dim, parts):
        steps = jax.random.uniform(jax.random.fold_in(jax.random.fold_in(key, 6), dim), (parts,), jnp.float32, low / len(shards), top_value / len(shards))
        return jnp.repeat(jnp.exp(steps), extent[dim] // parts).reshape((-1,) + (1,) * (len(extent) - dim - 1))

    loudness = one(*shards[0])
    for cut in shards[1:]:
        loudness = loudness * one(*cut)
    return loudness


def bell_draw(rng, dims, spread, most, split=(), held_as=jnp.bfloat16):
    values = jax.random.normal(rng, dims, jnp.float32) * spread
    if len(split) > 0:
        values = shard_levels(rng, dims, split, -0.22, 0.18) * values
    return jnp.clip(values, min=-most, max=most).astype(held_as)


def setup_inputs(seed: int = 0) -> dict:
    key_list = jax.random.split(jax.random.key(seed), 11)
    pair = bell_draw(key_list[0], (N, N, CZ), 1.0, 6.0, ((0, 256),))
    pair_mask = touch_ends((jax.random.randint(key_list[1], (N, N), 0, 8) < 7).astype(jnp.int32), jax.random.fold_in(key_list[1], 1), 0, 1)
    in_gain = jnp.clip(1.0 + 0.18 * jax.random.normal(key_list[2], (CZ,), jnp.float32), 0.1, 1.9)
    in_bias = bell_draw(key_list[3], (CZ,), 0.5, 3.0, (), jnp.float32)
    w_value = bell_draw(key_list[4], (CZ, 2 * CH), CZ ** -0.5, 0.5)
    w_gate = bell_draw(key_list[5], (CZ, 2 * CH), CZ ** -0.5, 0.5)
    out_gate_w = bell_draw(key_list[6], (CZ, CZ), CZ ** -0.5, 0.5)
    out_gain = jnp.clip(1.0 + 0.18 * jax.random.normal(key_list[7], (CH,), jnp.float32), 0.1, 1.9)
    out_bias = bell_draw(key_list[8], (CH,), 0.5, 3.0, (), jnp.float32)
    w_out = bell_draw(key_list[9], (CH, CZ), CH ** -0.5, 0.5)
    return dict(pair=pair, pair_mask=pair_mask, in_gain=in_gain, in_bias=in_bias, w_value=w_value, w_gate=w_gate, out_gate_w=out_gate_w, out_gain=out_gain, out_bias=out_bias, w_out=w_out)


eps_norm = 1e-05

def normalize(values, gain, bias, axis):
    average = lax.optimization_barrier(jnp.mean(values, axis=axis, keepdims=True))
    centred = values - average
    variance = lax.optimization_barrier(jnp.mean(centred * centred, axis=axis, keepdims=True))
    return centred * lax.rsqrt(variance + eps_norm) * gain + bias

def reference(pair, pair_mask, in_gain, in_bias, w_value, w_gate, out_gate_w, out_gain, out_bias, w_out):
    group_size = CH // N_CHAN
    block_data = pair.reshape(N_ROW, ROW_DEV, N, CZ)

    def norm_block(rows_in):
        return normalize(rows_in.astype(jnp.float32), in_gain, in_bias, -1).astype(jnp.bfloat16)
    normed = lax.map(norm_block, block_data)
    masks = pair_mask.reshape(N_ROW, ROW_DEV, N).astype(jnp.float32)
    block_ids = jnp.arange(N_ROW, dtype=jnp.int32)

    def one_group(group_id):
        first = (group_id * group_size).astype(jnp.int32)
        second = (CH + group_id * group_size).astype(jnp.int32)
        value_cols = jnp.concatenate([lax.dynamic_slice_in_dim(w_value, first, group_size, 1), lax.dynamic_slice_in_dim(w_value, second, group_size, 1)], 1)
        gate_cols = jnp.concatenate([lax.dynamic_slice_in_dim(w_gate, first, group_size, 1), lax.dynamic_slice_in_dim(w_gate, second, group_size, 1)], 1)

        def project(operands):
            rows_in, mask_rows = operands
            flat = rows_in.reshape(ROW_DEV * N, CZ)
            values = jnp.dot(flat, value_cols, preferred_element_type=jnp.float32)
            gate_pre = jnp.dot(flat, gate_cols, preferred_element_type=jnp.float32)
            mixed_ab = (jax.nn.sigmoid(gate_pre) * values).reshape(ROW_DEV, N, 2 * group_size) * mask_rows[:, :, None]
            return jnp.transpose(mixed_ab.astype(jnp.bfloat16), (0, 2, 1))
        mixed_all = lax.map(project, (normed, masks)).reshape(N, 2 * group_size, N)
        left_rows = mixed_all[:, :group_size]
        right_rows = mixed_all[:, group_size:]
        right_ext = jnp.concatenate([right_rows, right_rows[:WIN]], 0)

        def window(row_block):
            start = (row_block * ROW_DEV).astype(jnp.int32)
            left_block = lax.dynamic_slice_in_dim(left_rows, start, ROW_DEV, 0).astype(jnp.float32)
            right_band = lax.dynamic_slice_in_dim(right_ext, start, WIN, 0).astype(jnp.float32)
            return jnp.einsum('ikl,jkl->kij', left_block, right_band)
        return lax.map(window, block_ids)
    triangle = lax.map(one_group, jnp.arange(N_CHAN, dtype=jnp.int32))

    def finish(row_block):
        tri_block = triangle[:, row_block].reshape(CH, ROW_DEV, WIN)
        scaled = normalize(tri_block, out_gain[:, None, None], out_bias[:, None, None], 0).astype(jnp.bfloat16)
        projected = jnp.einsum('krm,ko->rmo', scaled.astype(jnp.float32), w_out.astype(jnp.float32))
        normed_block = normed[row_block]
        extended = jnp.concatenate([normed_block, normed_block[:, :WIN]], 1)
        window_rows = lax.dynamic_slice_in_dim(extended, (row_block * ROW_DEV).astype(jnp.int32), WIN, 1)
        out_gate = jax.nn.sigmoid(jnp.dot(window_rows.reshape(ROW_DEV * WIN, CZ), out_gate_w, preferred_element_type=jnp.float32)).reshape(ROW_DEV, WIN, CZ)
        return (projected * out_gate).astype(jnp.bfloat16)
    return lax.map(finish, block_ids).reshape(N, WIN, CZ)
```

```python
import functools

import jax
import jax.numpy as jnp
from jax import lax
from jax.experimental import pallas as pl
from jax.experimental.pallas import tpu as pltpu
from jax.sharding import Mesh, PartitionSpec as P

EPS = 1e-05
BLOCK = 64
STEPS = 4
SUB = 8
PLANE = ("yhi", "core", "x", "ylo")
PARTS = 32
OWN = 4
HALVES = ((0, 1024), (1024, 1024))
F32 = jnp.float32
BF16 = jnp.bfloat16
VMEM_LIMIT = 56 * 1024 * 1024


def dot(a, b, dims):
    return lax.dot_general(a, b, (dims, ((), ())), preferred_element_type=F32)


def columns(row):
    return jnp.transpose(jnp.broadcast_to(row, (128, 128)))


def across(block, width):
    return jnp.concatenate([block] * (width // 128), axis=1)


def project_kernel(pair_ref, mask_ref, gain_ref, bias_ref, value_ref, gate_ref, out_ref, mixed):
    width = pair_ref.shape[1]
    lane = lax.broadcasted_iota(jnp.int32, (128, 128), 0)
    sub = lax.broadcasted_iota(jnp.int32, (128, 128), 1)
    eye = jnp.where(lane == sub, 1.0, 0.0).astype(BF16)
    gain = across(columns(gain_ref[...]), width)
    bias = across(columns(bias_ref[...]), width)
    value_t = jnp.transpose(value_ref[...].astype(F32)).astype(BF16)
    gate_t = jnp.transpose(gate_ref[...].astype(F32) * 0.5).astype(BF16)
    weight = jnp.concatenate([value_t, gate_t], axis=0)
    half_mask = mask_ref[...].astype(F32) * 0.5
    for row in range(SUB):
        turned = dot(eye, pair_ref[row], ((1,), (1,)))
        centred = turned - jnp.sum(turned, axis=0, keepdims=True) * (1.0 / 128)
        variance = jnp.sum(centred * centred, axis=0, keepdims=True) * (1.0 / 128)
        normed = (centred * lax.rsqrt(variance + EPS) * gain + bias).astype(BF16)
        both = dot(weight, normed, ((1,), (0,)))
        half = both[:128] * half_mask[row : row + 1]
        result = half + half * jnp.tanh(both[128:])
        for tile in range(width // 128):
            first = (tile * SUB + row) * 128
            mixed[first : first + 128, :] = result[:, tile * 128 : (tile + 1) * 128]
    for tile in range(width // 128):
        for part in range(PARTS):
            first = tile * SUB * 128 + part * OWN
            pieces = [mixed[pl.ds(first + k, SUB, stride=128), :] for k in range(OWN)]
            out_ref[part, :, tile * 128 : (tile + 1) * 128] = jnp.concatenate(
                pieces, axis=0
            ).astype(BF16)


def project(pair, mask, gain, bias, w_value, w_gate, side, start, length):
    width = min(512, length)
    first = start // width
    whole = lambda i: (0, 0)
    column = lambda i: (0, side)
    tokens = SUB * length
    return pl.pallas_call(
        project_kernel,
        grid=(length // width,),
        in_specs=[
            pl.BlockSpec((SUB, width, 128), lambda i: (0, first + i, 0)),
            pl.BlockSpec((SUB, width), lambda i: (0, first + i)),
            pl.BlockSpec((1, 128), whole),
            pl.BlockSpec((1, 128), whole),
            pl.BlockSpec((128, 128), column),
            pl.BlockSpec((128, 128), column),
        ],
        out_specs=pl.BlockSpec((PARTS, OWN * SUB, width), lambda i: (0, 0, i)),
        out_shape=jax.ShapeDtypeStruct((PARTS, OWN * SUB, length), BF16),
        scratch_shapes=[pltpu.VMEM((SUB * width, 128), F32)],
        compiler_params=pltpu.CompilerParams(vmem_limit_bytes=VMEM_LIMIT),
        cost_estimate=pl.CostEstimate(
            flops=tokens * 128 * 384 * 2, bytes_accessed=tokens * 512, transcendentals=tokens * 128
        ),
        name="project",
    )(pair, mask, gain, bias, w_value, w_gate)


def rows_of(ref, pair_of_channels):
    parts, _, width = ref.shape
    both = ref[:, pair_of_channels * 16 : (pair_of_channels + 1) * 16, :].astype(F32)
    return [
        both[:, k * SUB : (k + 1) * SUB, :].reshape(parts * SUB, width).astype(BF16)
        for k in range(2)
    ]


def contract_kernel(last, left_ref, right_ref, next_ref, *rest):
    if last:
        before_ref, out_ref, total = rest
    else:
        out_ref, total = rest
    step = pl.program_id(0)

    @pl.when(step == 0)
    def _():
        total[...] = before_ref[...] if last else jnp.zeros_like(total)

    for pair_of_channels in range(OWN // 2):
        left = rows_of(left_ref, pair_of_channels)
        right = rows_of(right_ref, pair_of_channels)
        after = rows_of(next_ref, pair_of_channels)
        for k in range(2):
            window = jnp.concatenate([right[k], after[k]], axis=0)
            total[pair_of_channels * 2 + k] += dot(left[k], window, ((1,), (1,)))

    @pl.when(step == pl.num_programs(0) - 1)
    def _():
        if not last:
            out_ref[...] = total[...]
        else:
            groups = BLOCK // SUB
            for block in range(STEPS):
                for pair_of_channels in range(OWN // 2):
                    band = [
                        total[
                            pair_of_channels * 2 + k,
                            block * BLOCK : (block + 1) * BLOCK,
                            block * BLOCK : (block + STEPS) * BLOCK,
                        ].reshape(groups, SUB, STEPS * BLOCK)
                        for k in range(2)
                    ]
                    out_ref[
                        block * groups : (block + 1) * groups,
                        pair_of_channels * 16 : (pair_of_channels + 1) * 16,
                        :,
                    ] = jnp.concatenate(band, axis=1).astype(BF16)


def contract(left, right, after, before):
    length = left.shape[2]
    width = 256
    last = before is not None
    shape = (OWN, BLOCK * STEPS, BLOCK * (2 * STEPS - 1))
    part = lambda i: (0, 0, i)
    whole = lambda i: (0, 0, 0)
    in_specs = [pl.BlockSpec(v.shape[:2] + (width,), part) for v in (left, right, after)]
    operands = [left, right, after]
    if last:
        in_specs.append(pl.BlockSpec(shape, whole))
        operands.append(before)
        out_shape = jax.ShapeDtypeStruct((PARTS, OWN * SUB, STEPS * BLOCK), BF16)
    else:
        out_shape = jax.ShapeDtypeStruct(shape, F32)
    return pl.pallas_call(
        functools.partial(contract_kernel, last),
        grid=(length // width,),
        in_specs=in_specs,
        out_specs=pl.BlockSpec(out_shape.shape, whole),
        out_shape=out_shape,
        scratch_shapes=[pltpu.VMEM(shape, F32)],
        compiler_params=pltpu.CompilerParams(vmem_limit_bytes=VMEM_LIMIT),
        cost_estimate=pl.CostEstimate(
            flops=2 * 4 * 256 * 448 * length, bytes_accessed=6 * 1024 * length, transcendentals=0
        ),
        name="contract",
    )(*operands)


def finish_kernel(triangle_ref, gate_ref, gain_ref, bias_ref, w_ref, out_ref, scaled):
    width = triangle_ref.shape[2]
    values = triangle_ref[...].astype(F32).reshape(128, SUB, width)
    centred = values - jnp.sum(values, axis=0, keepdims=True) * (1.0 / 128)
    variance = jnp.sum(centred * centred, axis=0, keepdims=True) * (1.0 / 128)
    even = (centred * lax.rsqrt(variance + EPS)).reshape(128 * SUB, width)
    tiles = width // 128
    for tile in range(tiles):
        scaled[tile * SUB * 128 : (tile + 1) * SUB * 128, :] = even[:, tile * 128 : (tile + 1) * 128]
    gain = across(columns(gain_ref[...]), width)
    bias = across(columns(bias_ref[...]), width)
    for row in range(SUB):
        mine = [scaled[pl.ds(tile * SUB * 128 + row, 128, stride=SUB), :] for tile in range(tiles)]
        held = (jnp.concatenate(mine, axis=1) * gain + bias).astype(BF16)
        projected = dot(held, w_ref[...], ((0,), (0,)))
        out_ref[row] = (projected * gate_ref[row]).astype(BF16)


def finish(triangle, gate, gain, bias, w_out):
    width = 256
    whole = lambda i: (0, 0)
    return pl.pallas_call(
        finish_kernel,
        grid=(STEPS * BLOCK // width,),
        in_specs=[
            pl.BlockSpec((PARTS, OWN * SUB, width), lambda i: (0, 0, i)),
            pl.BlockSpec((SUB, width, 128), lambda i: (0, i, 0)),
            pl.BlockSpec((1, 128), whole),
            pl.BlockSpec((1, 128), whole),
            pl.BlockSpec((128, 128), whole),
        ],
        out_specs=pl.BlockSpec((SUB, width, 128), lambda i: (0, i, 0)),
        out_shape=jax.ShapeDtypeStruct((SUB, STEPS * BLOCK, 128), BF16),
        scratch_shapes=[pltpu.VMEM((SUB * width, 128), F32)],
        compiler_params=pltpu.CompilerParams(vmem_limit_bytes=VMEM_LIMIT),
        cost_estimate=pl.CostEstimate(
            flops=SUB * 256 * 128 * 256, bytes_accessed=2 * 1024 * 1024, transcendentals=2048
        ),
        name="finish",
    )(triangle, gate, gain, bias, w_out)


def output_gate(pair, in_gain, in_bias, out_gate_w, block):
    blocks = pair.shape[1] // BLOCK
    window = jnp.concatenate(
        [
            lax.dynamic_slice_in_dim(pair, lax.rem(block + k, blocks) * BLOCK, BLOCK, 1)
            for k in range(STEPS)
        ],
        axis=1,
    ).astype(F32)
    centred = window - jnp.mean(window, axis=-1, keepdims=True)
    variance = jnp.mean(centred * centred, axis=-1, keepdims=True)
    normed = (centred * lax.rsqrt(variance + EPS) * in_gain + in_bias).astype(BF16)
    return jax.nn.sigmoid(dot(normed, out_gate_w, ((2,), (0,))))


def on_device(
    pair, pair_mask, in_gain, in_bias, w_value, w_gate, out_gate_w, out_gain, out_bias, w_out
):
    gain, bias = in_gain.reshape(1, 128), in_bias.reshape(1, 128)
    planes = lax.axis_size("z")
    to_before = [(i, (i - 1) % planes) for i in range(planes)]

    def operand(side, chunk):
        return project(pair, pair_mask, gain, bias, w_value, w_gate, side, *chunk)

    def spread(value):
        return lax.all_to_all(value, PLANE, 0, 0, tiled=True)

    rights = [spread(operand(1, chunk)) for chunk in HALVES]
    afters = [
        lax.ppermute(right[: (STEPS - 1) * BLOCK // SUB], "z", to_before) for right in rights
    ]
    lefts = [spread(operand(0, chunk)) for chunk in HALVES]
    block = lax.axis_index("z") * 4 + lax.axis_index("yhi") * 2 + lax.axis_index("core")
    gate = output_gate(pair, in_gain, in_bias, out_gate_w, block)
    total = contract(lefts[0], rights[0], afters[0], None)
    band = contract(lefts[1], rights[1], afters[1], total)
    triangle = spread(band)
    return finish(triangle, gate, out_gain.reshape(1, 128), out_bias.reshape(1, 128), w_out)


def solution(mesh):
    fine = Mesh(mesh.devices.reshape(4, 2, 8, 2, 2), ("x", "ylo", "z", "yhi", "core"))
    rows = ("z", "yhi", "core", "x", "ylo")
    placed = (P(rows, None, None), P(rows, None)) + (P(),) * 8
    return jax.shard_map(
        on_device,
        mesh=fine,
        in_specs=placed,
        out_specs=P(rows, None, None),
        check_vma=False,
    )
```

```python
import functools

import jax
import jax.numpy as jnp
from jax import lax
from jax.experimental import pallas as pl
from jax.experimental.pallas import tpu as pltpu
from jax.sharding import Mesh, PartitionSpec as P

EPS = 1e-05
BLOCK = 64
STEPS = 4
SUB = 8
PLANE = ("yhi", "core", "x", "ylo")
PARTS = 32
OWN = 4
RIGHTS = ((0, 768), (768, 1280))
CHUNK = 256
STRIDE = 136
F32 = jnp.float32
BF16 = jnp.bfloat16
VMEM_LIMIT = 56 * 1024 * 1024


def dot(a, b, dims):
    return lax.dot_general(a, b, (dims, ((), ())), preferred_element_type=F32)


def columns(row):
    return jnp.transpose(jnp.broadcast_to(row, (128, 128)))


def across(block, width):
    return jnp.concatenate([block] * (width // 128), axis=1)


def project_kernel(pair_ref, mask_ref, gain_ref, bias_ref, value_ref, gate_ref, out_ref, mixed):
    width = pair_ref.shape[1]
    gain = across(columns(gain_ref[...]), CHUNK)
    bias = across(columns(bias_ref[...]), CHUNK)
    value_t = jnp.transpose(value_ref[...].astype(F32)).astype(BF16)
    gate_t = jnp.transpose(gate_ref[...].astype(F32) * 0.5).astype(BF16)
    weight = jnp.concatenate([value_t, gate_t], axis=0)
    for start in range(0, width, CHUNK):
        for row in range(SUB):
            turned = jnp.transpose(pair_ref[row, start : start + CHUNK, :]).astype(F32)
            half_mask = mask_ref[row : row + 1, start : start + CHUNK].astype(F32) * 0.5
            centred = turned - jnp.sum(turned, axis=0, keepdims=True) * (1.0 / 128)
            variance = jnp.sum(centred * centred, axis=0, keepdims=True) * (1.0 / 128)
            normed = (centred * lax.rsqrt(variance + EPS) * gain + bias).astype(BF16)
            both = dot(weight, normed, ((1,), (0,)))
            half = both[:128] * half_mask
            result = half + half * jnp.tanh(both[128:])
            for tile in range(CHUNK // 128):
                first = ((start // 128 + tile) * SUB + row) * STRIDE
                mixed[first : first + 128, :] = result[:, tile * 128 : (tile + 1) * 128]
        for tile in range(start // 128, (start + CHUNK) // 128):
            for part in range(PARTS):
                first = tile * SUB * STRIDE + part * OWN
                pieces = [mixed[pl.ds(first + k, SUB, stride=STRIDE), :] for k in range(OWN)]
                out_ref[part, :, tile * 128 : (tile + 1) * 128] = jnp.concatenate(
                    pieces, axis=0
                ).astype(BF16)


def project(pair, mask, gain, bias, w_value, w_gate, side, start, length):
    width = 512 if start % 512 == 0 and length % 512 == 0 else 256
    first = start // width
    whole = lambda i: (0, 0)
    column = lambda i: (0, side)
    tokens = SUB * length
    return pl.pallas_call(
        project_kernel,
        grid=(length // width,),
        in_specs=[
            pl.BlockSpec((SUB, width, 128), lambda i: (0, first + i, 0)),
            pl.BlockSpec((SUB, width), lambda i: (0, first + i)),
            pl.BlockSpec((1, 128), whole),
            pl.BlockSpec((1, 128), whole),
            pl.BlockSpec((128, 128), column),
            pl.BlockSpec((128, 128), column),
        ],
        out_specs=pl.BlockSpec((PARTS, OWN * SUB, width), lambda i: (0, 0, i)),
        out_shape=jax.ShapeDtypeStruct((PARTS, OWN * SUB, length), BF16),
        scratch_shapes=[pltpu.VMEM((SUB * STRIDE * (width // 128), 128), F32)],
        compiler_params=pltpu.CompilerParams(vmem_limit_bytes=VMEM_LIMIT),
        cost_estimate=pl.CostEstimate(
            flops=tokens * 128 * 384 * 2, bytes_accessed=tokens * 512, transcendentals=tokens * 128
        ),
        name="project",
    )(pair, mask, gain, bias, w_value, w_gate)


def rows_of(ref, pair_of_channels):
    parts, _, width = ref.shape
    both = ref[:, pair_of_channels * 16 : (pair_of_channels + 1) * 16, :].astype(F32)
    return [
        both[:, k * SUB : (k + 1) * SUB, :].reshape(parts * SUB, width).astype(BF16)
        for k in range(2)
    ]


def contract_kernel(steps, left_ref, *rest):
    pieces = rest[: 2 * len(steps)]
    out_ref, total = rest[2 * len(steps) :]
    step = pl.program_id(0)

    @pl.when(step == 0)
    def _():
        total[...] = jnp.zeros_like(total)

    for k, (begin, end) in enumerate(steps):

        @pl.when((step >= begin) & (step < end))
        def _(right_ref=pieces[2 * k], next_ref=pieces[2 * k + 1]):
            for pair_of_channels in range(OWN // 2):
                left = rows_of(left_ref, pair_of_channels)
                right = rows_of(right_ref, pair_of_channels)
                after = rows_of(next_ref, pair_of_channels)
                for k in range(2):
                    window = jnp.concatenate([right[k], after[k]], axis=0)
                    total[pair_of_channels * 2 + k] += dot(left[k], window, ((1,), (1,)))

    @pl.when(step == pl.num_programs(0) - 1)
    def _():
        groups = BLOCK // SUB
        for block in range(STEPS):
            for pair_of_channels in range(OWN // 2):
                band = [
                    total[
                        pair_of_channels * 2 + k,
                        block * BLOCK : (block + 1) * BLOCK,
                        block * BLOCK : (block + STEPS) * BLOCK,
                    ].reshape(groups, SUB, STEPS * BLOCK)
                    for k in range(2)
                ]
                out_ref[
                    block * groups : (block + 1) * groups,
                    pair_of_channels * 16 : (pair_of_channels + 1) * 16,
                    :,
                ] = jnp.concatenate(band, axis=1).astype(BF16)


def contract(left, pieces):
    length = left.shape[2]
    in_specs = [pl.BlockSpec(left.shape[:2] + (CHUNK,), lambda i: (0, 0, i))]
    operands, steps, begin = [left], [], 0
    for right, after in pieces:
        count = right.shape[2] // CHUNK
        place = lambda i, first=begin, most=count - 1: (0, 0, jnp.clip(i - first, 0, most))
        in_specs += [pl.BlockSpec(v.shape[:2] + (CHUNK,), place) for v in (right, after)]
        operands += [right, after]
        steps.append((begin, begin + count))
        begin += count
    out_shape = jax.ShapeDtypeStruct((PARTS, OWN * SUB, STEPS * BLOCK), BF16)
    return pl.pallas_call(
        functools.partial(contract_kernel, tuple(steps)),
        grid=(length // CHUNK,),
        in_specs=in_specs,
        out_specs=pl.BlockSpec(out_shape.shape, lambda i: (0, 0, 0)),
        out_shape=out_shape,
        scratch_shapes=[pltpu.VMEM((OWN, BLOCK * STEPS, BLOCK * (2 * STEPS - 1)), F32)],
        compiler_params=pltpu.CompilerParams(vmem_limit_bytes=VMEM_LIMIT),
        cost_estimate=pl.CostEstimate(
            flops=2 * 4 * 256 * 448 * length, bytes_accessed=6 * 1024 * length, transcendentals=0
        ),
        name="contract",
    )(*operands)


def finish_kernel(triangle_ref, gate_ref, gain_ref, bias_ref, w_ref, out_ref, scaled):
    width = triangle_ref.shape[2]
    values = triangle_ref[...].astype(F32).reshape(128, SUB, width)
    centred = values - jnp.sum(values, axis=0, keepdims=True) * (1.0 / 128)
    variance = jnp.sum(centred * centred, axis=0, keepdims=True) * (1.0 / 128)
    even = (centred * lax.rsqrt(variance + EPS)).reshape(128 * SUB, width)
    tiles = width // 128
    for tile in range(tiles):
        scaled[tile * SUB * 128 : (tile + 1) * SUB * 128, :] = even[:, tile * 128 : (tile + 1) * 128]
    gain = across(columns(gain_ref[...]), width)
    bias = across(columns(bias_ref[...]), width)
    for row in range(SUB):
        mine = [scaled[pl.ds(tile * SUB * 128 + row, 128, stride=SUB), :] for tile in range(tiles)]
        held = (jnp.concatenate(mine, axis=1) * gain + bias).astype(BF16)
        projected = dot(held, w_ref[...], ((0,), (0,)))
        out_ref[row] = (projected * gate_ref[row]).astype(BF16)


def finish(triangle, gate, gain, bias, w_out):
    width = 256
    whole = lambda i: (0, 0)
    return pl.pallas_call(
        finish_kernel,
        grid=(STEPS * BLOCK // width,),
        in_specs=[
            pl.BlockSpec((PARTS, OWN * SUB, width), lambda i: (0, 0, i)),
            pl.BlockSpec((SUB, width, 128), lambda i: (0, i, 0)),
            pl.BlockSpec((1, 128), whole),
            pl.BlockSpec((1, 128), whole),
            pl.BlockSpec((128, 128), whole),
        ],
        out_specs=pl.BlockSpec((SUB, width, 128), lambda i: (0, i, 0)),
        out_shape=jax.ShapeDtypeStruct((SUB, STEPS * BLOCK, 128), BF16),
        scratch_shapes=[pltpu.VMEM((SUB * width, 128), F32)],
        compiler_params=pltpu.CompilerParams(vmem_limit_bytes=VMEM_LIMIT),
        cost_estimate=pl.CostEstimate(
            flops=SUB * 256 * 128 * 256, bytes_accessed=2 * 1024 * 1024, transcendentals=2048
        ),
        name="finish",
    )(triangle, gate, gain, bias, w_out)


def output_gate(pair, in_gain, in_bias, out_gate_w, block):
    blocks = pair.shape[1] // BLOCK
    window = jnp.concatenate(
        [
            lax.dynamic_slice_in_dim(pair, lax.rem(block + k, blocks) * BLOCK, BLOCK, 1)
            for k in range(STEPS)
        ],
        axis=1,
    ).astype(F32)
    centred = window - jnp.mean(window, axis=-1, keepdims=True)
    variance = jnp.mean(centred * centred, axis=-1, keepdims=True)
    normed = (centred * lax.rsqrt(variance + EPS) * in_gain + in_bias).astype(BF16)
    return jax.nn.sigmoid(dot(normed, out_gate_w, ((2,), (0,))))


def on_device(
    pair, pair_mask, in_gain, in_bias, w_value, w_gate, out_gate_w, out_gain, out_bias, w_out
):
    gain, bias = in_gain.reshape(1, 128), in_bias.reshape(1, 128)
    planes = lax.axis_size("z")
    to_before = [(i, (i - 1) % planes) for i in range(planes)]

    def operand(side, chunk):
        return project(pair, pair_mask, gain, bias, w_value, w_gate, side, *chunk)

    def spread(value):
        return lax.all_to_all(value, PLANE, 0, 0, tiled=True)

    def shifted(right):
        return lax.ppermute(right[: (STEPS - 1) * BLOCK // SUB], "z", to_before)

    first = spread(operand(1, RIGHTS[0]))
    first_after = shifted(first)
    second = spread(operand(1, RIGHTS[1]))
    second_after = shifted(second)
    left = operand(0, (0, pair.shape[1]))
    left, first_after = lax.optimization_barrier((left, first_after))
    left = spread(left)
    block = lax.axis_index("z") * 4 + lax.axis_index("yhi") * 2 + lax.axis_index("core")
    gate = output_gate(pair, in_gain, in_bias, out_gate_w, block)
    triangle = spread(contract(left, [(first, first_after), (second, second_after)]))
    return finish(triangle, gate, out_gain.reshape(1, 128), out_bias.reshape(1, 128), w_out)


def solution(mesh):
    fine = Mesh(mesh.devices.reshape(4, 2, 8, 2, 2), ("x", "ylo", "z", "yhi", "core"))
    rows = ("z", "yhi", "core", "x", "ylo")
    placed = (P(rows, None, None), P(rows, None)) + (P(),) * 8
    return jax.shard_map(
        on_device,
        mesh=fine,
        in_specs=placed,
        out_specs=P(rows, None, None),
        check_vma=False,
    )
```

```python
import functools

import jax
import jax.numpy as jnp
from jax import lax
from jax.experimental import pallas as pl
from jax.experimental.pallas import tpu as pltpu
from jax.sharding import Mesh, PartitionSpec as P

EPS = 1e-05
BLOCK = 64
STEPS = 4
SUB = 8
PLANE = ("yhi", "core", "x", "ylo")
PARTS = 32
OWN = 4
RIGHTS = ((0, 640), (640, 1408))
CHUNK = 128
STRIDE = 136
F32 = jnp.float32
BF16 = jnp.bfloat16
VMEM_LIMIT = 24 * 1024 * 1024
VMEM_CONTRACT = 36 * 1024 * 1024
VMEM_FIRST = 60 * 1024 * 1024


def dot(a, b, dims):
    return lax.dot_general(a, b, (dims, ((), ())), preferred_element_type=F32)


def columns(row):
    return jnp.transpose(jnp.broadcast_to(row, (128, 128)))


def across(block, width):
    return jnp.concatenate([block] * (width // 128), axis=1)


def project_kernel(pair_ref, mask_ref, gain_ref, bias_ref, value_ref, gate_ref, out_ref, mixed):
    width = pair_ref.shape[1]
    gain = across(columns(gain_ref[...]), CHUNK)
    bias = across(columns(bias_ref[...]), CHUNK)
    value_t = jnp.transpose(value_ref[...].astype(F32)).astype(BF16)
    gate_t = jnp.transpose(gate_ref[...].astype(F32) * 0.5).astype(BF16)
    weight = jnp.concatenate([value_t, gate_t], axis=0)
    for start in range(0, width, CHUNK):
        for row in range(SUB):
            turned = jnp.transpose(pair_ref[row, start : start + CHUNK, :]).astype(F32)
            half_mask = mask_ref[row : row + 1, start : start + CHUNK].astype(F32) * 0.5
            centred = turned - jnp.sum(turned, axis=0, keepdims=True) * (1.0 / 128)
            variance = jnp.sum(centred * centred, axis=0, keepdims=True) * (1.0 / 128)
            normed = (centred * lax.rsqrt(variance + EPS) * gain + bias).astype(BF16)
            both = dot(weight, normed, ((1,), (0,)))
            half = both[:128] * half_mask
            result = half + half * jnp.tanh(both[128:])
            for tile in range(CHUNK // 128):
                first = ((start // 128 + tile) * SUB + row) * STRIDE
                mixed[first : first + 128, :] = result[:, tile * 128 : (tile + 1) * 128]
        for tile in range(start // 128, (start + CHUNK) // 128):
            for part in range(PARTS):
                first = tile * SUB * STRIDE + part * OWN
                pieces = [mixed[pl.ds(first + k, SUB, stride=STRIDE), :] for k in range(OWN)]
                out_ref[part, :, tile * 128 : (tile + 1) * 128] = jnp.concatenate(
                    pieces, axis=0
                ).astype(BF16)


def project(pair, mask, gain, bias, w_value, w_gate, side, start, length):
    width = max(w for w in range(128, 641, 128) if start % w == 0 and length % w == 0)
    first = start // width
    whole = lambda i: (0, 0)
    column = lambda i: (0, side)
    tokens = SUB * length
    return pl.pallas_call(
        project_kernel,
        grid=(length // width,),
        in_specs=[
            pl.BlockSpec((SUB, width, 128), lambda i: (0, first + i, 0)),
            pl.BlockSpec((SUB, width), lambda i: (0, first + i)),
            pl.BlockSpec((1, 128), whole),
            pl.BlockSpec((1, 128), whole),
            pl.BlockSpec((128, 128), column),
            pl.BlockSpec((128, 128), column),
        ],
        out_specs=pl.BlockSpec((PARTS, OWN * SUB, width), lambda i: (0, 0, i)),
        out_shape=jax.ShapeDtypeStruct((PARTS, OWN * SUB, length), BF16),
        scratch_shapes=[pltpu.VMEM((SUB * STRIDE * (width // 128), 128), F32)],
        compiler_params=pltpu.CompilerParams(
            vmem_limit_bytes=VMEM_FIRST if side == 1 and start == 0 else VMEM_LIMIT
        ),
        cost_estimate=pl.CostEstimate(
            flops=tokens * 128 * 384 * 2, bytes_accessed=tokens * 512, transcendentals=tokens * 128
        ),
        name="project",
    )(pair, mask, gain, bias, w_value, w_gate)


def rows_of(ref, pair_of_channels):
    parts, _, width = ref.shape
    both = ref[:, pair_of_channels * 16 : (pair_of_channels + 1) * 16, :].astype(F32)
    return [
        both[:, k * SUB : (k + 1) * SUB, :].reshape(parts * SUB, width).astype(BF16)
        for k in range(2)
    ]


def contract_kernel(steps, left_hbm, *rest):
    count = len(steps)
    pieces, out_ref, left_ref = rest[: 2 * count], rest[2 * count], rest[2 * count + 1]
    held = rest[2 * count + 2 : 4 * count + 2]
    total, sems = rest[4 * count + 2 :]
    copies = []
    for k, (begin, length) in enumerate(steps):
        tokens = pl.ds(begin, length)
        mine = [
            pltpu.make_async_copy(
                left_hbm.at[:, :, tokens], left_ref.at[:, :, tokens], sems.at[3 * k]
            )
        ] + [
            pltpu.make_async_copy(pieces[2 * k + j], held[2 * k + j], sems.at[3 * k + 1 + j])
            for j in range(2)
        ]
        for copy in mine:
            copy.start()
        copies.append(mine)
    groups = BLOCK // SUB
    for k, (begin, length) in enumerate(steps):
        for copy in copies[k]:
            copy.wait()
        for pair_of_channels in range(OWN // 2):
            left = rows_of(left_ref.at[:, :, pl.ds(begin, length)], pair_of_channels)
            right = rows_of(held[2 * k], pair_of_channels)
            after = rows_of(held[2 * k + 1], pair_of_channels)
            for j in range(2):
                window = jnp.concatenate([right[j], after[j]], axis=0)
                product = dot(left[j], window, ((1,), (1,)))
                channel = pair_of_channels * 2 + j
                total[channel] = product if k == 0 else total[channel] + product
            if k < count - 1:
                continue
            for block in range(STEPS):
                band = [
                    total[
                        pair_of_channels * 2 + j,
                        block * BLOCK : (block + 1) * BLOCK,
                        block * BLOCK : (block + STEPS) * BLOCK,
                    ].reshape(groups, SUB, STEPS * BLOCK)
                    for j in range(2)
                ]
                out_ref[
                    block * groups : (block + 1) * groups,
                    pair_of_channels * 16 : (pair_of_channels + 1) * 16,
                    :,
                ] = jnp.concatenate(band, axis=1).astype(BF16)


def contract(left, pieces):
    operands, steps, begin = [left], [], 0
    for right, after in pieces:
        operands += [right, after]
        steps.append((begin, right.shape[2]))
        begin += right.shape[2]
    return pl.pallas_call(
        functools.partial(contract_kernel, tuple(steps)),
        in_specs=[pl.BlockSpec(memory_space=pl.ANY)] * len(operands),
        out_specs=pl.BlockSpec(memory_space=pltpu.VMEM),
        out_shape=jax.ShapeDtypeStruct((PARTS, OWN * SUB, STEPS * BLOCK), BF16),
        scratch_shapes=[pltpu.VMEM(v.shape, BF16) for v in operands]
        + [
            pltpu.VMEM((OWN, BLOCK * STEPS, BLOCK * (2 * STEPS - 1)), F32),
            pltpu.SemaphoreType.DMA((3 * len(pieces),)),
        ],
        compiler_params=pltpu.CompilerParams(vmem_limit_bytes=VMEM_CONTRACT),
        cost_estimate=pl.CostEstimate(
            flops=2 * 4 * 256 * 448 * left.shape[2],
            bytes_accessed=6 * 1024 * left.shape[2],
            transcendentals=0,
        ),
        name="contract",
    )(*operands)


def finish_kernel(triangle_ref, gate_ref, gain_ref, bias_ref, w_ref, out_ref, scaled):
    width = triangle_ref.shape[2]
    values = triangle_ref[...].astype(F32).reshape(128, SUB, width)
    centred = values - jnp.sum(values, axis=0, keepdims=True) * (1.0 / 128)
    variance = jnp.sum(centred * centred, axis=0, keepdims=True) * (1.0 / 128)
    even = (centred * lax.rsqrt(variance + EPS)).reshape(128 * SUB, width)
    tiles = width // 128
    for tile in range(tiles):
        scaled[tile * SUB * 128 : (tile + 1) * SUB * 128, :] = even[:, tile * 128 : (tile + 1) * 128]
    gain = across(columns(gain_ref[...]), width)
    bias = across(columns(bias_ref[...]), width)
    for row in range(SUB):
        mine = [scaled[pl.ds(tile * SUB * 128 + row, 128, stride=SUB), :] for tile in range(tiles)]
        held = (jnp.concatenate(mine, axis=1) * gain + bias).astype(BF16)
        projected = dot(held, w_ref[...], ((0,), (0,)))
        out_ref[row] = (projected * gate_ref[row]).astype(BF16)


def finish(triangle, gate, gain, bias, w_out):
    width = 256
    whole = lambda i: (0, 0)
    return pl.pallas_call(
        finish_kernel,
        grid=(STEPS * BLOCK // width,),
        in_specs=[
            pl.BlockSpec((PARTS, OWN * SUB, width), lambda i: (0, 0, i)),
            pl.BlockSpec((SUB, width, 128), lambda i: (0, i, 0)),
            pl.BlockSpec((1, 128), whole),
            pl.BlockSpec((1, 128), whole),
            pl.BlockSpec((128, 128), whole),
        ],
        out_specs=pl.BlockSpec((SUB, width, 128), lambda i: (0, i, 0)),
        out_shape=jax.ShapeDtypeStruct((SUB, STEPS * BLOCK, 128), BF16),
        scratch_shapes=[pltpu.VMEM((SUB * width, 128), F32)],
        compiler_params=pltpu.CompilerParams(vmem_limit_bytes=VMEM_LIMIT),
        cost_estimate=pl.CostEstimate(
            flops=SUB * 256 * 128 * 256, bytes_accessed=2 * 1024 * 1024, transcendentals=2048
        ),
        name="finish",
    )(triangle, gate, gain, bias, w_out)


def gate_kernel(block_ref, p0, p1, p2, p3, gain_ref, bias_ref, w_ref, out_ref):
    for k, ref in enumerate((p0, p1, p2, p3)):
        rows = ref[...].reshape(SUB * BLOCK, 128).astype(F32)
        centred = rows - jnp.sum(rows, axis=1, keepdims=True) * (1.0 / 128)
        variance = jnp.sum(centred * centred, axis=1, keepdims=True) * (1.0 / 128)
        normed = centred * lax.rsqrt(variance + EPS) * gain_ref[...] + bias_ref[...]
        half = dot(normed.astype(BF16), w_ref[...], ((1,), (0,))) * 0.5
        out_ref[:, k * BLOCK : (k + 1) * BLOCK, :] = (jnp.tanh(half) * 0.5 + 0.5).reshape(
            SUB, BLOCK, 128
        )


def output_gate(pair, gain, bias, out_gate_w, block):
    blocks = pair.shape[1] // BLOCK
    whole = lambda i, first: (0, 0)
    spec = pltpu.PrefetchScalarGridSpec(
        num_scalar_prefetch=1,
        grid=(1,),
        in_specs=[
            pl.BlockSpec(
                (SUB, BLOCK, 128), lambda i, first, k=k: (0, lax.rem(first[0] + k, blocks), 0)
            )
            for k in range(STEPS)
        ]
        + [
            pl.BlockSpec((1, 128), whole),
            pl.BlockSpec((1, 128), whole),
            pl.BlockSpec((128, 128), whole),
        ],
        out_specs=pl.BlockSpec((SUB, STEPS * BLOCK, 128), lambda i, first: (0, 0, 0)),
    )
    return pl.pallas_call(
        gate_kernel,
        grid_spec=spec,
        out_shape=jax.ShapeDtypeStruct((SUB, STEPS * BLOCK, 128), F32),
        compiler_params=pltpu.CompilerParams(vmem_limit_bytes=VMEM_LIMIT),
        cost_estimate=pl.CostEstimate(
            flops=SUB * 256 * 128 * 256, bytes_accessed=2 * 1024 * 1024, transcendentals=2**18
        ),
        name="gate",
    )(block.astype(jnp.int32).reshape(1), pair, pair, pair, pair, gain, bias, out_gate_w)


def on_device(
    pair, pair_mask, in_gain, in_bias, w_value, w_gate, out_gate_w, out_gain, out_bias, w_out
):
    gain, bias = in_gain.reshape(1, 128), in_bias.reshape(1, 128)
    planes = lax.axis_size("z")
    to_before = [(i, (i - 1) % planes) for i in range(planes)]

    def operand(side, chunk):
        return project(pair, pair_mask, gain, bias, w_value, w_gate, side, *chunk)

    def spread(value):
        return lax.all_to_all(value, PLANE, 0, 0, tiled=True)

    def shifted(right):
        return lax.ppermute(right[: (STEPS - 1) * BLOCK // SUB], "z", to_before)

    first = spread(operand(1, RIGHTS[0]))
    first_after = shifted(first)
    second = spread(operand(1, RIGHTS[1]))
    second_after = shifted(second)
    left = operand(0, (0, pair.shape[1]))
    left, first_after = lax.optimization_barrier((left, first_after))
    left = spread(left)
    block = lax.axis_index("z") * 4 + lax.axis_index("yhi") * 2 + lax.axis_index("core")
    gate = output_gate(pair, gain, bias, out_gate_w, block)
    first, gate = lax.optimization_barrier((first, gate))
    triangle = spread(contract(left, [(first, first_after), (second, second_after)]))
    return finish(triangle, gate, out_gain.reshape(1, 128), out_bias.reshape(1, 128), w_out)


def solution(mesh):
    fine = Mesh(mesh.devices.reshape(4, 2, 8, 2, 2), ("x", "ylo", "z", "yhi", "core"))
    rows = ("z", "yhi", "core", "x", "ylo")
    placed = (P(rows, None, None), P(rows, None)) + (P(),) * 8
    return jax.shard_map(
        on_device,
        mesh=fine,
        in_specs=placed,
        out_specs=P(rows, None, None),
        check_vma=False,
    )
```

```python
import functools

import jax
import jax.numpy as jnp
from jax import lax
from jax.experimental import pallas as pl
from jax.experimental.pallas import tpu as pltpu
from jax.sharding import Mesh, PartitionSpec as P

EPS = 1e-05
BLOCK = 64
STEPS = 4
SUB = 8
PLANE = ("yhi", "core", "x", "ylo")
PARTS = 32
OWN = 4
RIGHTS = ((0, 768), (768, 1280))
CHUNK = 128
STRIDE = 136
F32 = jnp.float32
BF16 = jnp.bfloat16
VMEM_LIMIT = 60 * 1024 * 1024
VMEM_SMALL = 24 * 1024 * 1024


def dot(a, b, dims):
    return lax.dot_general(a, b, (dims, ((), ())), preferred_element_type=F32)


def columns(row):
    return jnp.transpose(jnp.broadcast_to(row, (128, 128)))


def across(block, width):
    return jnp.concatenate([block] * (width // 128), axis=1)


def projection(gain_ref, bias_ref, value_ref, gate_ref):
    gain = across(columns(gain_ref[...]), CHUNK)
    bias = across(columns(bias_ref[...]), CHUNK)
    value_t = jnp.transpose(value_ref[...].astype(F32)).astype(BF16)
    gate_t = jnp.transpose(gate_ref[...].astype(F32) * 0.5).astype(BF16)
    return gain, bias, jnp.concatenate([value_t, gate_t], axis=0)


def project_chunk(params, pair_ref, mask_ref, out_ref, mixed, start):
    gain, bias, weight = params
    for row in range(SUB):
        turned = jnp.transpose(pair_ref[row, start : start + CHUNK, :]).astype(F32)
        half_mask = mask_ref[row : row + 1, start : start + CHUNK].astype(F32) * 0.5
        centred = turned - jnp.sum(turned, axis=0, keepdims=True) * (1.0 / 128)
        variance = jnp.sum(centred * centred, axis=0, keepdims=True) * (1.0 / 128)
        normed = (centred * lax.rsqrt(variance + EPS) * gain + bias).astype(BF16)
        both = dot(weight, normed, ((1,), (0,)))
        half = both[:128] * half_mask
        first = (start // CHUNK * SUB + row) * STRIDE
        mixed[first : first + 128, :] = half + half * jnp.tanh(both[128:])
    for part in range(PARTS):
        first = start // CHUNK * SUB * STRIDE + part * OWN
        pieces = [mixed[pl.ds(first + k, SUB, stride=STRIDE), :] for k in range(OWN)]
        out_ref[part, :, start : start + CHUNK] = jnp.concatenate(pieces, axis=0).astype(BF16)


def project_kernel(pair_ref, mask_ref, gain_ref, bias_ref, value_ref, gate_ref, out_ref, mixed):
    params = projection(gain_ref, bias_ref, value_ref, gate_ref)
    for start in range(0, pair_ref.shape[1], CHUNK):
        project_chunk(params, pair_ref, mask_ref, out_ref, mixed, start)


def project(pair, mask, gain, bias, w_value, w_gate, side, start, length):
    width = max(w for w in range(CHUNK, 513, CHUNK) if start % w == 0 and length % w == 0)
    first = start // width
    whole = lambda i: (0, 0)
    column = lambda i: (0, side)
    tokens = SUB * length
    return pl.pallas_call(
        project_kernel,
        grid=(length // width,),
        in_specs=[
            pl.BlockSpec((SUB, width, 128), lambda i: (0, first + i, 0)),
            pl.BlockSpec((SUB, width), lambda i: (0, first + i)),
            pl.BlockSpec((1, 128), whole),
            pl.BlockSpec((1, 128), whole),
            pl.BlockSpec((128, 128), column),
            pl.BlockSpec((128, 128), column),
        ],
        out_specs=pl.BlockSpec((PARTS, OWN * SUB, width), lambda i: (0, 0, i)),
        out_shape=jax.ShapeDtypeStruct((PARTS, OWN * SUB, length), BF16),
        scratch_shapes=[pltpu.VMEM((SUB * STRIDE * (width // CHUNK), 128), F32)],
        compiler_params=pltpu.CompilerParams(
            vmem_limit_bytes=VMEM_LIMIT if side == 1 and start == 0 else VMEM_SMALL
        ),
        cost_estimate=pl.CostEstimate(
            flops=tokens * 128 * 384 * 2, bytes_accessed=tokens * 512, transcendentals=tokens * 128
        ),
        name="project",
    )(pair, mask, gain, bias, w_value, w_gate)


def rows_of(ref, pair_of_channels):
    parts, _, width = ref.shape
    both = ref[:, pair_of_channels * 16 : (pair_of_channels + 1) * 16, :].astype(F32)
    return [
        both[:, k * SUB : (k + 1) * SUB, :].reshape(parts * SUB, width).astype(BF16)
        for k in range(2)
    ]


def contract_kernel(steps, left_hbm, *rest):
    count, halves = len(steps), OWN // 2
    pieces, out_ref, left_ref = rest[: 2 * count], rest[2 * count], rest[2 * count + 1]
    held = rest[2 * count + 2 : 4 * count + 2]
    total, sems = rest[4 * count + 2 :]
    copies = {}
    for k, (begin, length) in enumerate(steps):
        tokens = pl.ds(begin, length)
        for half in range(halves):
            rows = pl.ds(half * 16, 16)
            sem = 3 * (k * halves + half)
            copies[k, half] = [
                pltpu.make_async_copy(
                    left_hbm.at[:, rows, tokens], left_ref.at[:, rows, tokens], sems.at[sem]
                )
            ] + [
                pltpu.make_async_copy(
                    pieces[2 * k + j].at[:, rows, :], held[2 * k + j].at[:, rows, :], sems.at[sem + 1 + j]
                )
                for j in range(2)
            ]
            for copy in copies[k, half]:
                copy.start()
    groups = BLOCK // SUB
    for k, (begin, length) in enumerate(steps):
        for pair_of_channels in range(halves):
            for copy in copies[k, pair_of_channels]:
                copy.wait()
            left = rows_of(left_ref.at[:, :, pl.ds(begin, length)], pair_of_channels)
            right = rows_of(held[2 * k], pair_of_channels)
            after = rows_of(held[2 * k + 1], pair_of_channels)
            for j in range(2):
                window = jnp.concatenate([right[j], after[j]], axis=0)
                product = dot(left[j], window, ((1,), (1,)))
                channel = pair_of_channels * 2 + j
                total[channel] = product if k == 0 else total[channel] + product
            if k < count - 1:
                continue
            for block in range(STEPS):
                band = [
                    total[
                        pair_of_channels * 2 + j,
                        block * BLOCK : (block + 1) * BLOCK,
                        block * BLOCK : (block + STEPS) * BLOCK,
                    ].reshape(groups, SUB, STEPS * BLOCK)
                    for j in range(2)
                ]
                out_ref[
                    block * groups : (block + 1) * groups,
                    pair_of_channels * 16 : (pair_of_channels + 1) * 16,
                    :,
                ] = jnp.concatenate(band, axis=1).astype(BF16)


def contract(left, pieces):
    operands, steps, begin = [left], [], 0
    for right, after in pieces:
        operands += [right, after]
        steps.append((begin, right.shape[2]))
        begin += right.shape[2]
    return pl.pallas_call(
        functools.partial(contract_kernel, tuple(steps)),
        in_specs=[pl.BlockSpec(memory_space=pltpu.HBM)] * len(operands),
        out_specs=pl.BlockSpec(memory_space=pltpu.VMEM),
        out_shape=jax.ShapeDtypeStruct((PARTS, OWN * SUB, STEPS * BLOCK), BF16),
        scratch_shapes=[pltpu.VMEM(v.shape, BF16) for v in operands]
        + [
            pltpu.VMEM((OWN, BLOCK * STEPS, BLOCK * (2 * STEPS - 1)), F32),
            pltpu.SemaphoreType.DMA((3 * OWN // 2 * len(pieces),)),
        ],
        compiler_params=pltpu.CompilerParams(vmem_limit_bytes=VMEM_LIMIT),
        cost_estimate=pl.CostEstimate(
            flops=2 * 4 * 256 * 448 * left.shape[2],
            bytes_accessed=6 * 1024 * left.shape[2],
            transcendentals=0,
        ),
        name="contract",
    )(*operands)


def finish_kernel(triangle_ref, gate_ref, gain_ref, bias_ref, w_ref, out_ref, scaled):
    width = triangle_ref.shape[2]
    values = triangle_ref[...].astype(F32).reshape(128, SUB, width)
    centred = values - jnp.sum(values, axis=0, keepdims=True) * (1.0 / 128)
    variance = jnp.sum(centred * centred, axis=0, keepdims=True) * (1.0 / 128)
    even = (centred * lax.rsqrt(variance + EPS)).reshape(128 * SUB, width)
    tiles = width // 128
    for tile in range(tiles):
        scaled[tile * SUB * 128 : (tile + 1) * SUB * 128, :] = even[:, tile * 128 : (tile + 1) * 128]
    gain = across(columns(gain_ref[...]), width)
    bias = across(columns(bias_ref[...]), width)
    for row in range(SUB):
        mine = [scaled[pl.ds(tile * SUB * 128 + row, 128, stride=SUB), :] for tile in range(tiles)]
        held = (jnp.concatenate(mine, axis=1) * gain + bias).astype(BF16)
        projected = dot(held, w_ref[...], ((0,), (0,)))
        out_ref[row] = (projected * gate_ref[row]).astype(BF16)


def finish(triangle, gate, gain, bias, w_out):
    width = 256
    whole = lambda i: (0, 0)
    return pl.pallas_call(
        finish_kernel,
        grid=(STEPS * BLOCK // width,),
        in_specs=[
            pl.BlockSpec((PARTS, OWN * SUB, width), lambda i: (0, 0, i)),
            pl.BlockSpec((SUB, width, 128), lambda i: (0, i, 0)),
            pl.BlockSpec((1, 128), whole),
            pl.BlockSpec((1, 128), whole),
            pl.BlockSpec((128, 128), whole),
        ],
        out_specs=pl.BlockSpec((SUB, width, 128), lambda i: (0, i, 0)),
        out_shape=jax.ShapeDtypeStruct((SUB, STEPS * BLOCK, 128), BF16),
        scratch_shapes=[pltpu.VMEM((SUB * width, 128), F32)],
        compiler_params=pltpu.CompilerParams(vmem_limit_bytes=VMEM_SMALL),
        cost_estimate=pl.CostEstimate(
            flops=SUB * 256 * 128 * 256, bytes_accessed=2 * 1024 * 1024, transcendentals=2048
        ),
        name="finish",
    )(triangle, gate, gain, bias, w_out)


def gate_kernel(block_ref, p0, p1, p2, p3, gain_ref, bias_ref, w_ref, out_ref):
    for k, ref in enumerate((p0, p1, p2, p3)):
        rows = ref[...].reshape(SUB * BLOCK, 128).astype(F32)
        centred = rows - jnp.sum(rows, axis=1, keepdims=True) * (1.0 / 128)
        variance = jnp.sum(centred * centred, axis=1, keepdims=True) * (1.0 / 128)
        normed = centred * lax.rsqrt(variance + EPS) * gain_ref[...] + bias_ref[...]
        half = dot(normed.astype(BF16), w_ref[...], ((1,), (0,))) * 0.5
        out_ref[:, k * BLOCK : (k + 1) * BLOCK, :] = (jnp.tanh(half) * 0.5 + 0.5).reshape(
            SUB, BLOCK, 128
        )


def output_gate(pair, gain, bias, out_gate_w, block):
    blocks = pair.shape[1] // BLOCK
    whole = lambda i, first: (0, 0)
    spec = pltpu.PrefetchScalarGridSpec(
        num_scalar_prefetch=1,
        grid=(1,),
        in_specs=[
            pl.BlockSpec(
                (SUB, BLOCK, 128), lambda i, first, k=k: (0, lax.rem(first[0] + k, blocks), 0)
            )
            for k in range(STEPS)
        ]
        + [
            pl.BlockSpec((1, 128), whole),
            pl.BlockSpec((1, 128), whole),
            pl.BlockSpec((128, 128), whole),
        ],
        out_specs=pl.BlockSpec((SUB, STEPS * BLOCK, 128), lambda i, first: (0, 0, 0)),
    )
    return pl.pallas_call(
        gate_kernel,
        grid_spec=spec,
        out_shape=jax.ShapeDtypeStruct((SUB, STEPS * BLOCK, 128), F32),
        compiler_params=pltpu.CompilerParams(vmem_limit_bytes=VMEM_SMALL),
        cost_estimate=pl.CostEstimate(
            flops=SUB * 256 * 128 * 256, bytes_accessed=2 * 1024 * 1024, transcendentals=2**18
        ),
        name="gate",
    )(block.astype(jnp.int32).reshape(1), pair, pair, pair, pair, gain, bias, out_gate_w)


def on_device(
    pair, pair_mask, in_gain, in_bias, w_value, w_gate, out_gate_w, out_gain, out_bias, w_out
):
    gain, bias = in_gain.reshape(1, 128), in_bias.reshape(1, 128)
    planes = lax.axis_size("z")
    to_before = [(i, (i - 1) % planes) for i in range(planes)]

    def operand(side, chunk):
        return project(pair, pair_mask, gain, bias, w_value, w_gate, side, *chunk)

    def spread(value):
        return lax.all_to_all(value, PLANE, 0, 0, tiled=True)

    def shifted(right):
        return lax.ppermute(right[: (STEPS - 1) * BLOCK // SUB], "z", to_before)

    first = spread(operand(1, RIGHTS[0]))
    first_after = shifted(first)
    second = spread(operand(1, RIGHTS[1]))
    second_after = shifted(second)
    left = operand(0, (0, pair.shape[1]))
    left, first_after = lax.optimization_barrier((left, first_after))
    left = spread(left)
    block = lax.axis_index("z") * 4 + lax.axis_index("yhi") * 2 + lax.axis_index("core")
    band = contract(left, [(first, first_after), (second, second_after)])
    band, block = lax.optimization_barrier((band, block))
    gate = output_gate(pair, gain, bias, out_gate_w, block)
    triangle = spread(band)
    return finish(triangle, gate, out_gain.reshape(1, 128), out_bias.reshape(1, 128), w_out)


def solution(mesh):
    fine = Mesh(mesh.devices.reshape(4, 2, 8, 2, 2), ("x", "ylo", "z", "yhi", "core"))
    rows = ("z", "yhi", "core", "x", "ylo")
    placed = (P(rows, None, None), P(rows, None)) + (P(),) * 8
    return jax.shard_map(
        on_device,
        mesh=fine,
        in_specs=placed,
        out_specs=P(rows, None, None),
        check_vma=False,
    )
```

```python
import functools

import jax
import jax.numpy as jnp
from jax import lax
from jax.experimental import pallas as pl
from jax.experimental.pallas import tpu as pltpu
from jax.sharding import Mesh, PartitionSpec as P

EPS = 1e-05
BLOCK = 64
STEPS = 4
SUB = 8
PLANE = ("yhi", "core", "x", "ylo")
PARTS = 32
OWN = 4
DOTS = ((0, 768), (768, 1280))
CHUNK = 128
STRIDE = 130
F32 = jnp.float32
BF16 = jnp.bfloat16
VMEM_LIMIT = 60 * 1024 * 1024
VMEM_SMALL = 24 * 1024 * 1024


def dot(a, b, dims):
    return lax.dot_general(a, b, (dims, ((), ())), preferred_element_type=F32)


def columns(row):
    return jnp.transpose(jnp.broadcast_to(row, (128, 128)))


def across(block, width):
    return jnp.concatenate([block] * (width // 128), axis=1)


def projection(gain_ref, bias_ref, value_ref, gate_ref):
    gain = across(columns(gain_ref[...]), CHUNK)
    bias = across(columns(bias_ref[...]), CHUNK)
    value_t = jnp.transpose(value_ref[...].astype(F32)).astype(BF16)
    gate_t = jnp.transpose(gate_ref[...].astype(F32) * 0.5).astype(BF16)
    return gain, bias, jnp.concatenate([value_t, gate_t], axis=0)


def project_chunk(params, pair_ref, mask_ref, out_ref, mixed, start):
    gain, bias, weight = params
    for row in range(SUB):
        turned = jnp.transpose(pair_ref[row, start : start + CHUNK, :]).astype(F32)
        half_mask = mask_ref[row : row + 1, start : start + CHUNK].astype(F32) * 0.5
        centred = turned - jnp.sum(turned, axis=0, keepdims=True) * (1.0 / 128)
        variance = jnp.sum(centred * centred, axis=0, keepdims=True) * (1.0 / 128)
        normed = (centred * lax.rsqrt(variance + EPS) * gain + bias).astype(BF16)
        both = dot(weight, normed, ((1,), (0,)))
        half = both[:128] * half_mask
        first = (start // CHUNK * SUB + row) * STRIDE
        mixed[first : first + 128, :] = half + half * jnp.tanh(both[128:])
    for part in range(PARTS):
        first = start // CHUNK * SUB * STRIDE + part * OWN
        pieces = [mixed[pl.ds(first + k, SUB, stride=STRIDE), :] for k in range(OWN)]
        out_ref[part, :, start : start + CHUNK] = jnp.concatenate(pieces, axis=0).astype(BF16)


def project_kernel(side_ref, pair_ref, mask_ref, gain_ref, bias_ref, value_ref, gate_ref, out_ref, mixed):
    params = projection(gain_ref, bias_ref, value_ref, gate_ref)
    for start in range(0, pair_ref.shape[1], CHUNK):
        project_chunk(params, pair_ref, mask_ref, out_ref, mixed, start)


def project(pair, mask, gain, bias, w_value, w_gate, side, limit):
    length = pair.shape[1]
    width = 512
    tokens = SUB * length
    whole = lambda i, side: (0, 0)
    column = lambda i, side: (0, side[0])
    spec = pltpu.PrefetchScalarGridSpec(
        num_scalar_prefetch=1,
        grid=(length // width,),
        in_specs=[
            pl.BlockSpec((SUB, width, 128), lambda i, side: (0, i, 0)),
            pl.BlockSpec((SUB, width), lambda i, side: (0, i)),
            pl.BlockSpec((1, 128), whole),
            pl.BlockSpec((1, 128), whole),
            pl.BlockSpec((128, 128), column),
            pl.BlockSpec((128, 128), column),
        ],
        out_specs=pl.BlockSpec((PARTS, OWN * SUB, width), lambda i, side: (0, 0, i)),
        scratch_shapes=[pltpu.VMEM((SUB * STRIDE * (width // CHUNK), 128), F32)],
    )
    return pl.pallas_call(
        project_kernel,
        grid_spec=spec,
        out_shape=jax.ShapeDtypeStruct((PARTS, OWN * SUB, length), BF16),
        compiler_params=pltpu.CompilerParams(vmem_limit_bytes=limit),
        cost_estimate=pl.CostEstimate(
            flops=tokens * 128 * 384 * 2, bytes_accessed=tokens * 512, transcendentals=tokens * 128
        ),
        name="project",
    )(side.reshape(1), pair, mask, gain, bias, w_value, w_gate)


def rows_of(ref, parts, tokens, half):
    both = ref[parts, half * 16 : (half + 1) * 16, tokens].astype(F32)
    count, _, width = both.shape
    return [
        both[:, k * SUB : (k + 1) * SUB, :].reshape(count * SUB, width).astype(BF16)
        for k in range(2)
    ]


def corner_kernel(left_ref, right_ref, out_ref):
    every = slice(None)
    for half in range(OWN // 2):
        left = rows_of(left_ref, every, every, half)
        right = rows_of(right_ref, every, every, half)
        for k in range(2):
            out_ref[half * 2 + k] = dot(left[k], right[k], ((1,), (1,)))


def corner(left, early):
    shape = left.shape
    return pl.pallas_call(
        corner_kernel,
        grid=(1,),
        in_specs=[
            pl.BlockSpec(shape, lambda i: (0, 0, 0)),
            pl.BlockSpec(shape, lambda i: (STEPS - 2, 0, 0)),
        ],
        out_specs=pl.BlockSpec((OWN, BLOCK, BLOCK), lambda i: (0, 0, 0)),
        out_shape=jax.ShapeDtypeStruct((OWN, BLOCK, BLOCK), F32),
        compiler_params=pltpu.CompilerParams(vmem_limit_bytes=VMEM_SMALL),
        cost_estimate=pl.CostEstimate(
            flops=2 * 4 * 64 * 64 * 2048, bytes_accessed=2 * 1024 * 1024, transcendentals=0
        ),
        name="corner",
    )(left, early)


def contract_kernel(
    early_hbm, late_hbm, after_hbm, corner_hbm, out_ref, early, late, after, corner_ref, total, sems, corner_sem
):
    halves = OWN // 2
    pairs = ((early_hbm, early), (late_hbm, late), (after_hbm, after))
    copies = {}
    for k, tokens in enumerate(DOTS):
        for half in range(halves):
            rows = pl.ds(half * 16, 16)
            copies[k, half] = [
                pltpu.make_async_copy(
                    source.at[:, rows, pl.ds(*tokens)],
                    target.at[:, rows, pl.ds(*tokens)],
                    sems.at[k * halves + half, j],
                )
                for j, (source, target) in enumerate(pairs)
            ]
            for copy in copies[k, half]:
                copy.start()
    corner_copy = pltpu.make_async_copy(corner_hbm, corner_ref, corner_sem)
    corner_copy.start()
    groups = BLOCK // SUB
    rest = slice(0, (STEPS - 1) * groups)
    last = slice((STEPS - 1) * groups, STEPS * groups)
    for k, (begin, length) in enumerate(DOTS):
        tokens = slice(begin, begin + length)
        for half in range(halves):
            for copy in copies[k, half]:
                copy.wait()
            early_rest, early_last = (rows_of(early, p, tokens, half) for p in (rest, last))
            late_rest, late_last = (rows_of(late, p, tokens, half) for p in (rest, last))
            following = rows_of(after, slice(None), tokens, half)
            for j in range(2):
                left = jnp.concatenate([late_rest[j], early_last[j]], axis=0)
                window = jnp.concatenate([early_rest[j], late_last[j], following[j]], axis=0)
                product = dot(left, window, ((1,), (1,)))
                channel = half * 2 + j
                total[channel] = product if k == 0 else total[channel] + product
            if k < len(DOTS) - 1:
                continue
            if half == 0:
                corner_copy.wait()
            for block in range(STEPS):
                band = []
                for channel in (half * 2, half * 2 + 1):
                    rows = total[
                        channel, block * BLOCK : (block + 1) * BLOCK, block * BLOCK : (block + STEPS) * BLOCK
                    ]
                    if block == STEPS - 1:
                        rows = jnp.concatenate([rows, corner_ref[channel]], axis=1)
                    band.append(rows.reshape(groups, SUB, STEPS * BLOCK))
                out_ref[
                    block * groups : (block + 1) * groups, half * 16 : (half + 1) * 16, :
                ] = jnp.concatenate(band, axis=1).astype(BF16)


def contract(early, late, after, returned):
    hbm = pl.BlockSpec(memory_space=pltpu.HBM)
    vmem = pl.BlockSpec(memory_space=pltpu.VMEM)
    window = BLOCK * (2 * STEPS - 2)
    return pl.pallas_call(
        contract_kernel,
        in_specs=[hbm] * 4,
        out_specs=vmem,
        out_shape=jax.ShapeDtypeStruct((PARTS, OWN * SUB, STEPS * BLOCK), BF16),
        scratch_shapes=[pltpu.VMEM(v.shape, BF16) for v in (early, late, after)]
        + [
            pltpu.VMEM(returned.shape, F32),
            pltpu.VMEM((OWN, BLOCK * STEPS, window), F32),
            pltpu.SemaphoreType.DMA((OWN // 2 * len(DOTS), 3)),
            pltpu.SemaphoreType.DMA(()),
        ],
        compiler_params=pltpu.CompilerParams(vmem_limit_bytes=VMEM_LIMIT),
        cost_estimate=pl.CostEstimate(
            flops=2 * 4 * 256 * window * 2048, bytes_accessed=11 * 2**20, transcendentals=0
        ),
        name="contract",
    )(early, late, after, returned)


def finish_kernel(triangle_ref, gate_ref, gain_ref, bias_ref, w_ref, out_ref, scaled):
    width = triangle_ref.shape[2]
    values = triangle_ref[...].astype(F32).reshape(128, SUB, width)
    centred = values - jnp.sum(values, axis=0, keepdims=True) * (1.0 / 128)
    variance = jnp.sum(centred * centred, axis=0, keepdims=True) * (1.0 / 128)
    even = (centred * lax.rsqrt(variance + EPS)).reshape(128 * SUB, width)
    tiles = width // 128
    for tile in range(tiles):
        scaled[tile * SUB * 128 : (tile + 1) * SUB * 128, :] = even[:, tile * 128 : (tile + 1) * 128]
    gain = across(columns(gain_ref[...]), width)
    bias = across(columns(bias_ref[...]), width)
    for row in range(SUB):
        mine = [scaled[pl.ds(tile * SUB * 128 + row, 128, stride=SUB), :] for tile in range(tiles)]
        held = (jnp.concatenate(mine, axis=1) * gain + bias).astype(BF16)
        projected = dot(held, w_ref[...], ((0,), (0,)))
        out_ref[row] = (projected * gate_ref[row]).astype(BF16)


def finish(triangle, gate, gain, bias, w_out):
    width = 256
    whole = lambda i: (0, 0)
    return pl.pallas_call(
        finish_kernel,
        grid=(STEPS * BLOCK // width,),
        in_specs=[
            pl.BlockSpec((PARTS, OWN * SUB, width), lambda i: (0, 0, i)),
            pl.BlockSpec((SUB, width, 128), lambda i: (0, i, 0)),
            pl.BlockSpec((1, 128), whole),
            pl.BlockSpec((1, 128), whole),
            pl.BlockSpec((128, 128), whole),
        ],
        out_specs=pl.BlockSpec((SUB, width, 128), lambda i: (0, i, 0)),
        out_shape=jax.ShapeDtypeStruct((SUB, STEPS * BLOCK, 128), BF16),
        scratch_shapes=[pltpu.VMEM((SUB * width, 128), F32)],
        compiler_params=pltpu.CompilerParams(vmem_limit_bytes=VMEM_SMALL),
        cost_estimate=pl.CostEstimate(
            flops=SUB * 256 * 128 * 256, bytes_accessed=2 * 1024 * 1024, transcendentals=2048
        ),
        name="finish",
    )(triangle, gate, gain, bias, w_out)


def gate_kernel(block_ref, p0, p1, p2, p3, gain_ref, bias_ref, w_ref, out_ref):
    for k, ref in enumerate((p0, p1, p2, p3)):
        rows = ref[...].reshape(SUB * BLOCK, 128).astype(F32)
        centred = rows - jnp.sum(rows, axis=1, keepdims=True) * (1.0 / 128)
        variance = jnp.sum(centred * centred, axis=1, keepdims=True) * (1.0 / 128)
        normed = centred * lax.rsqrt(variance + EPS) * gain_ref[...] + bias_ref[...]
        half = dot(normed.astype(BF16), w_ref[...], ((1,), (0,))) * 0.5
        out_ref[:, k * BLOCK : (k + 1) * BLOCK, :] = (jnp.tanh(half) * 0.5 + 0.5).reshape(
            SUB, BLOCK, 128
        )


def output_gate(pair, gain, bias, out_gate_w, block):
    blocks = pair.shape[1] // BLOCK
    whole = lambda i, first: (0, 0)
    spec = pltpu.PrefetchScalarGridSpec(
        num_scalar_prefetch=1,
        grid=(1,),
        in_specs=[
            pl.BlockSpec(
                (SUB, BLOCK, 128), lambda i, first, k=k: (0, lax.rem(first[0] + k, blocks), 0)
            )
            for k in range(STEPS)
        ]
        + [
            pl.BlockSpec((1, 128), whole),
            pl.BlockSpec((1, 128), whole),
            pl.BlockSpec((128, 128), whole),
        ],
        out_specs=pl.BlockSpec((SUB, STEPS * BLOCK, 128), lambda i, first: (0, 0, 0)),
    )
    return pl.pallas_call(
        gate_kernel,
        grid_spec=spec,
        out_shape=jax.ShapeDtypeStruct((SUB, STEPS * BLOCK, 128), F32),
        compiler_params=pltpu.CompilerParams(vmem_limit_bytes=VMEM_SMALL),
        cost_estimate=pl.CostEstimate(
            flops=SUB * 256 * 128 * 256, bytes_accessed=2 * 1024 * 1024, transcendentals=2**18
        ),
        name="gate",
    )(block.astype(jnp.int32).reshape(1), pair, pair, pair, pair, gain, bias, out_gate_w)


def on_device(
    pair, pair_mask, in_gain, in_bias, w_value, w_gate, out_gate_w, out_gain, out_bias, w_out
):
    gain, bias = in_gain.reshape(1, 128), in_bias.reshape(1, 128)
    planes = lax.axis_size("z")
    down = [(i, (i - 1) % planes) for i in range(planes)]
    up = [(i, (i + 1) % planes) for i in range(planes)]
    place = lax.axis_index("yhi") * 2 + lax.axis_index("core")
    block = lax.axis_index("z") * STEPS + place
    groups = BLOCK // SUB

    def operand(side, limit):
        return project(pair, pair_mask, gain, bias, w_value, w_gate, side, limit)

    def spread(value):
        return lax.all_to_all(value, PLANE, 0, 0, tiled=True)

    side = jnp.where(place == STEPS - 1, 0, 1).astype(jnp.int32)
    early = spread(operand(side, VMEM_LIMIT))
    above = lax.ppermute(early[(STEPS - 1) * groups :], "z", up)
    after = lax.ppermute(early[: 2 * groups], "z", down)
    returned = lax.ppermute(corner(above, early), "z", down)
    late = spread(operand(1 - side, VMEM_SMALL))
    band = contract(early, late, after, returned)
    band, block = lax.optimization_barrier((band, block))
    gate = output_gate(pair, gain, bias, out_gate_w, block)
    triangle = spread(band)
    return finish(triangle, gate, out_gain.reshape(1, 128), out_bias.reshape(1, 128), w_out)


def solution(mesh):
    fine = Mesh(mesh.devices.reshape(4, 2, 8, 2, 2), ("x", "ylo", "z", "yhi", "core"))
    rows = ("z", "yhi", "core", "x", "ylo")
    placed = (P(rows, None, None), P(rows, None)) + (P(),) * 8
    return jax.shard_map(
        on_device,
        mesh=fine,
        in_specs=placed,
        out_specs=P(rows, None, None),
        check_vma=False,
    )
```

```python
import functools

import jax
import jax.numpy as jnp
from jax import lax
from jax.experimental import pallas as pl
from jax.experimental.pallas import tpu as pltpu
from jax.sharding import Mesh, PartitionSpec as P

EPS = 1e-05
BLOCK = 64
STEPS = 4
SUB = 8
PLANE = ("yhi", "core", "x", "ylo")
PARTS = 32
OWN = 4
DOTS = ((0, 768), (768, 1280))
CHUNK = 128
STRIDE = 130
F32 = jnp.float32
BF16 = jnp.bfloat16
VMEM_LIMIT = 60 * 1024 * 1024
VMEM_SMALL = 24 * 1024 * 1024
VMEM_CONTRACT = 52 * 1024 * 1024


def dot(a, b, dims):
    return lax.dot_general(a, b, (dims, ((), ())), preferred_element_type=F32)


def columns(row):
    return jnp.transpose(jnp.broadcast_to(row, (128, 128)))


def across(block, width):
    return jnp.concatenate([block] * (width // 128), axis=1)


def projection(gain_ref, bias_ref, value_ref, gate_ref):
    gain = across(columns(gain_ref[...]), CHUNK)
    bias = across(columns(bias_ref[...]), CHUNK)
    value_t = jnp.transpose(value_ref[...].astype(F32)).astype(BF16)
    gate_t = jnp.transpose(gate_ref[...].astype(F32) * 0.5).astype(BF16)
    return gain, bias, jnp.concatenate([value_t, gate_t], axis=0)


def project_chunk(params, pair_ref, mask_ref, out_ref, mixed, start):
    gain, bias, weight = params
    for row in range(SUB):
        turned = jnp.transpose(pair_ref[row, start : start + CHUNK, :]).astype(F32)
        half_mask = mask_ref[row : row + 1, start : start + CHUNK].astype(F32) * 0.5
        centred = turned - jnp.sum(turned, axis=0, keepdims=True) * (1.0 / 128)
        variance = jnp.sum(centred * centred, axis=0, keepdims=True) * (1.0 / 128)
        normed = (centred * lax.rsqrt(variance + EPS) * gain + bias).astype(BF16)
        both = dot(weight, normed, ((1,), (0,)))
        half = both[:128] * half_mask
        first = (start // CHUNK * SUB + row) * STRIDE
        mixed[first : first + 128, :] = half + half * jnp.tanh(both[128:])
    for part in range(PARTS):
        first = start // CHUNK * SUB * STRIDE + part * OWN
        pieces = [mixed[pl.ds(first + k, SUB, stride=STRIDE), :] for k in range(OWN)]
        out_ref[part, :, start : start + CHUNK] = jnp.concatenate(pieces, axis=0).astype(BF16)


def project_kernel(side_ref, pair_ref, mask_ref, gain_ref, bias_ref, value_ref, gate_ref, out_ref, mixed):
    params = projection(gain_ref, bias_ref, value_ref, gate_ref)
    for start in range(0, pair_ref.shape[1], CHUNK):
        project_chunk(params, pair_ref, mask_ref, out_ref, mixed, start)


def project(pair, mask, gain, bias, w_value, w_gate, side, limit):
    length = pair.shape[1]
    width = 512
    tokens = SUB * length
    whole = lambda i, side: (0, 0)
    column = lambda i, side: (0, side[0])
    spec = pltpu.PrefetchScalarGridSpec(
        num_scalar_prefetch=1,
        grid=(length // width,),
        in_specs=[
            pl.BlockSpec((SUB, width, 128), lambda i, side: (0, i, 0)),
            pl.BlockSpec((SUB, width), lambda i, side: (0, i)),
            pl.BlockSpec((1, 128), whole),
            pl.BlockSpec((1, 128), whole),
            pl.BlockSpec((128, 128), column),
            pl.BlockSpec((128, 128), column),
        ],
        out_specs=pl.BlockSpec((PARTS, OWN * SUB, width), lambda i, side: (0, 0, i)),
        scratch_shapes=[pltpu.VMEM((SUB * STRIDE * (width // CHUNK), 128), F32)],
    )
    return pl.pallas_call(
        project_kernel,
        grid_spec=spec,
        out_shape=jax.ShapeDtypeStruct((PARTS, OWN * SUB, length), BF16),
        compiler_params=pltpu.CompilerParams(vmem_limit_bytes=limit),
        cost_estimate=pl.CostEstimate(
            flops=tokens * 128 * 384 * 2, bytes_accessed=tokens * 512, transcendentals=tokens * 128
        ),
        name="project",
    )(side.reshape(1), pair, mask, gain, bias, w_value, w_gate)


def rows_of(ref, parts, tokens, half):
    both = ref[parts, half * 16 : (half + 1) * 16, tokens].astype(F32)
    count, _, width = both.shape
    return [
        both[:, k * SUB : (k + 1) * SUB, :].reshape(count * SUB, width).astype(BF16)
        for k in range(2)
    ]


def corner_kernel(left_ref, right_ref, out_ref):
    every = slice(None)
    for half in range(OWN // 2):
        left = rows_of(left_ref, every, every, half)
        right = rows_of(right_ref, every, every, half)
        for k in range(2):
            product = dot(left[k], right[k], ((1,), (1,)))
            out_ref[half * 2 + k] = jnp.concatenate(
                [product[: BLOCK // 2], product[BLOCK // 2 :]], axis=1
            ).astype(BF16)


def corner(left, early):
    shape = left.shape
    return pl.pallas_call(
        corner_kernel,
        grid=(1,),
        in_specs=[
            pl.BlockSpec(shape, lambda i: (0, 0, 0)),
            pl.BlockSpec(shape, lambda i: (STEPS - 2, 0, 0)),
        ],
        out_specs=pl.BlockSpec((OWN, BLOCK // 2, 2 * BLOCK), lambda i: (0, 0, 0)),
        out_shape=jax.ShapeDtypeStruct((OWN, BLOCK // 2, 2 * BLOCK), BF16),
        compiler_params=pltpu.CompilerParams(vmem_limit_bytes=VMEM_SMALL),
        cost_estimate=pl.CostEstimate(
            flops=2 * 4 * 64 * 64 * 2048, bytes_accessed=2 * 1024 * 1024, transcendentals=0
        ),
        name="corner",
    )(left, early)


def contract_kernel(
    early_hbm, late_hbm, after_hbm, corner_hbm, out_ref, early, late, after, corner_ref, total, sems, corner_sem
):
    halves = OWN // 2
    pairs = ((early_hbm, early), (late_hbm, late), (after_hbm, after))
    copies = {}
    for k, tokens in enumerate(DOTS):
        for half in range(halves):
            rows = pl.ds(half * 16, 16)
            copies[k, half] = [
                pltpu.make_async_copy(
                    source.at[:, rows, pl.ds(*tokens)],
                    target.at[:, rows, pl.ds(*tokens)],
                    sems.at[k * halves + half, j],
                )
                for j, (source, target) in enumerate(pairs)
            ]
            for copy in copies[k, half]:
                copy.start()
    corner_copy = pltpu.make_async_copy(corner_hbm, corner_ref, corner_sem)
    corner_copy.start()
    groups = BLOCK // SUB
    rest = slice(0, (STEPS - 1) * groups)
    last = slice((STEPS - 1) * groups, STEPS * groups)
    for k, (begin, length) in enumerate(DOTS):
        tokens = slice(begin, begin + length)
        for half in range(halves):
            for copy in copies[k, half]:
                copy.wait()
            early_rest, early_last = (rows_of(early, p, tokens, half) for p in (rest, last))
            late_rest, late_last = (rows_of(late, p, tokens, half) for p in (rest, last))
            following = rows_of(after, slice(None), tokens, half)
            for j in range(2):
                left = jnp.concatenate([late_rest[j], early_last[j]], axis=0)
                window = jnp.concatenate([early_rest[j], late_last[j], following[j]], axis=0)
                product = dot(left, window, ((1,), (1,)))
                channel = half * 2 + j
                total[channel] = product if k == 0 else total[channel] + product
            if k < len(DOTS) - 1:
                continue
            if half == 0:
                corner_copy.wait()
            for block in range(STEPS):
                band = []
                for channel in (half * 2, half * 2 + 1):
                    rows = total[
                        channel, block * BLOCK : (block + 1) * BLOCK, block * BLOCK : (block + STEPS) * BLOCK
                    ]
                    if block == STEPS - 1:
                        folded = corner_ref[channel].astype(F32)
                        final = jnp.concatenate([folded[:, :BLOCK], folded[:, BLOCK:]], axis=0)
                        rows = jnp.concatenate([rows, final], axis=1)
                    band.append(rows.reshape(groups, SUB, STEPS * BLOCK))
                out_ref[
                    block * groups : (block + 1) * groups, half * 16 : (half + 1) * 16, :
                ] = jnp.concatenate(band, axis=1).astype(BF16)


def contract(early, late, after, returned):
    hbm = pl.BlockSpec(memory_space=pltpu.HBM)
    anywhere = pl.BlockSpec(memory_space=pl.ANY)
    vmem = pl.BlockSpec(memory_space=pltpu.VMEM)
    window = BLOCK * (2 * STEPS - 2)
    return pl.pallas_call(
        contract_kernel,
        in_specs=[hbm, hbm, anywhere, anywhere],
        out_specs=vmem,
        out_shape=jax.ShapeDtypeStruct((PARTS, OWN * SUB, STEPS * BLOCK), BF16),
        scratch_shapes=[pltpu.VMEM(v.shape, BF16) for v in (early, late, after)]
        + [
            pltpu.VMEM(returned.shape, BF16),
            pltpu.VMEM((OWN, BLOCK * STEPS, window), F32),
            pltpu.SemaphoreType.DMA((OWN // 2 * len(DOTS), 3)),
            pltpu.SemaphoreType.DMA(()),
        ],
        compiler_params=pltpu.CompilerParams(vmem_limit_bytes=VMEM_CONTRACT),
        cost_estimate=pl.CostEstimate(
            flops=2 * 4 * 256 * window * 2048, bytes_accessed=11 * 2**20, transcendentals=0
        ),
        name="contract",
    )(early, late, after, returned)


def finish_kernel(triangle_ref, gate_ref, gain_ref, bias_ref, w_ref, out_ref, scaled):
    width = triangle_ref.shape[2]
    values = triangle_ref[...].astype(F32).reshape(128, SUB, width)
    centred = values - jnp.sum(values, axis=0, keepdims=True) * (1.0 / 128)
    variance = jnp.sum(centred * centred, axis=0, keepdims=True) * (1.0 / 128)
    even = (centred * lax.rsqrt(variance + EPS)).reshape(128 * SUB, width)
    tiles = width // 128
    for tile in range(tiles):
        scaled[tile * SUB * 128 : (tile + 1) * SUB * 128, :] = even[:, tile * 128 : (tile + 1) * 128]
    gain = across(columns(gain_ref[...]), width)
    bias = across(columns(bias_ref[...]), width)
    for row in range(SUB):
        mine = [scaled[pl.ds(tile * SUB * 128 + row, 128, stride=SUB), :] for tile in range(tiles)]
        held = (jnp.concatenate(mine, axis=1) * gain + bias).astype(BF16)
        projected = dot(held, w_ref[...], ((0,), (0,)))
        out_ref[row] = (projected * gate_ref[row]).astype(BF16)


def finish(triangle, gate, gain, bias, w_out):
    width = 256
    whole = lambda i: (0, 0)
    return pl.pallas_call(
        finish_kernel,
        grid=(STEPS * BLOCK // width,),
        in_specs=[
            pl.BlockSpec((PARTS, OWN * SUB, width), lambda i: (0, 0, i)),
            pl.BlockSpec((SUB, width, 128), lambda i: (0, i, 0)),
            pl.BlockSpec((1, 128), whole),
            pl.BlockSpec((1, 128), whole),
            pl.BlockSpec((128, 128), whole),
        ],
        out_specs=pl.BlockSpec((SUB, width, 128), lambda i: (0, i, 0)),
        out_shape=jax.ShapeDtypeStruct((SUB, STEPS * BLOCK, 128), BF16),
        scratch_shapes=[pltpu.VMEM((SUB * width, 128), F32)],
        compiler_params=pltpu.CompilerParams(vmem_limit_bytes=VMEM_SMALL),
        cost_estimate=pl.CostEstimate(
            flops=SUB * 256 * 128 * 256, bytes_accessed=2 * 1024 * 1024, transcendentals=2048
        ),
        name="finish",
    )(triangle, gate, gain, bias, w_out)


def gate_kernel(block_ref, p0, p1, p2, p3, gain_ref, bias_ref, w_ref, out_ref):
    for k, ref in enumerate((p0, p1, p2, p3)):
        rows = ref[...].reshape(SUB * BLOCK, 128).astype(F32)
        centred = rows - jnp.sum(rows, axis=1, keepdims=True) * (1.0 / 128)
        variance = jnp.sum(centred * centred, axis=1, keepdims=True) * (1.0 / 128)
        normed = centred * lax.rsqrt(variance + EPS) * gain_ref[...] + bias_ref[...]
        half = dot(normed.astype(BF16), w_ref[...], ((1,), (0,))) * 0.5
        out_ref[:, k * BLOCK : (k + 1) * BLOCK, :] = (jnp.tanh(half) * 0.5 + 0.5).reshape(
            SUB, BLOCK, 128
        )


def output_gate(pair, gain, bias, out_gate_w, block):
    blocks = pair.shape[1] // BLOCK
    whole = lambda i, first: (0, 0)
    spec = pltpu.PrefetchScalarGridSpec(
        num_scalar_prefetch=1,
        grid=(1,),
        in_specs=[
            pl.BlockSpec(
                (SUB, BLOCK, 128), lambda i, first, k=k: (0, lax.rem(first[0] + k, blocks), 0)
            )
            for k in range(STEPS)
        ]
        + [
            pl.BlockSpec((1, 128), whole),
            pl.BlockSpec((1, 128), whole),
            pl.BlockSpec((128, 128), whole),
        ],
        out_specs=pl.BlockSpec((SUB, STEPS * BLOCK, 128), lambda i, first: (0, 0, 0)),
    )
    return pl.pallas_call(
        gate_kernel,
        grid_spec=spec,
        out_shape=jax.ShapeDtypeStruct((SUB, STEPS * BLOCK, 128), F32),
        compiler_params=pltpu.CompilerParams(vmem_limit_bytes=VMEM_SMALL),
        cost_estimate=pl.CostEstimate(
            flops=SUB * 256 * 128 * 256, bytes_accessed=2 * 1024 * 1024, transcendentals=2**18
        ),
        name="gate",
    )(block.astype(jnp.int32).reshape(1), pair, pair, pair, pair, gain, bias, out_gate_w)


def on_device(
    pair, pair_mask, in_gain, in_bias, w_value, w_gate, out_gate_w, out_gain, out_bias, w_out
):
    gain, bias = in_gain.reshape(1, 128), in_bias.reshape(1, 128)
    planes = lax.axis_size("z")
    down = [(i, (i - 1) % planes) for i in range(planes)]
    up = [(i, (i + 1) % planes) for i in range(planes)]
    place = lax.axis_index("yhi") * 2 + lax.axis_index("core")
    block = lax.axis_index("z") * STEPS + place
    groups = BLOCK // SUB

    def operand(side, limit):
        return project(pair, pair_mask, gain, bias, w_value, w_gate, side, limit)

    def spread(value):
        return lax.all_to_all(value, PLANE, 0, 0, tiled=True)

    side = jnp.where(place == STEPS - 1, 0, 1).astype(jnp.int32)
    early = spread(operand(side, VMEM_LIMIT))
    above = lax.ppermute(early[(STEPS - 1) * groups :], "z", up)
    after = lax.ppermute(early[: 2 * groups], "z", down)
    returned = lax.ppermute(corner(above, early), "z", down)
    late = spread(operand(1 - side, VMEM_SMALL))
    band = contract(early, late, after, returned)
    band, block = lax.optimization_barrier((band, block))
    gate = output_gate(pair, gain, bias, out_gate_w, block)
    triangle = spread(band)
    return finish(triangle, gate, out_gain.reshape(1, 128), out_bias.reshape(1, 128), w_out)


def solution(mesh):
    fine = Mesh(mesh.devices.reshape(4, 2, 8, 2, 2), ("x", "ylo", "z", "yhi", "core"))
    rows = ("z", "yhi", "core", "x", "ylo")
    placed = (P(rows, None, None), P(rows, None)) + (P(),) * 8
    return jax.shard_map(
        on_device,
        mesh=fine,
        in_specs=placed,
        out_specs=P(rows, None, None),
        check_vma=False,
    )
```

```python
import functools

import jax
import jax.numpy as jnp
from jax import lax
from jax.experimental import pallas as pl
from jax.experimental.pallas import tpu as pltpu
from jax.sharding import Mesh, PartitionSpec as P

EPS = 1e-05
BLOCK = 64
STEPS = 4
SUB = 8
PLANE = ("yhi", "core", "x", "ylo")
PARTS = 32
OWN = 4
DOTS = ((0, 768), (768, 1280))
CHUNK = 128
STRIDE = 130
F32 = jnp.float32
BF16 = jnp.bfloat16
VMEM_LIMIT = 60 * 1024 * 1024
VMEM_SMALL = 24 * 1024 * 1024
VMEM_CONTRACT = 52 * 1024 * 1024


def dot(a, b, dims):
    return lax.dot_general(a, b, (dims, ((), ())), preferred_element_type=F32)


def columns(row):
    return jnp.transpose(jnp.broadcast_to(row, (128, 128)))


def across(block, width):
    return jnp.concatenate([block] * (width // 128), axis=1)


def projection(gain_ref, bias_ref, value_ref, gate_ref):
    gain = across(columns(gain_ref[...]), CHUNK)
    bias = across(columns(bias_ref[...]), CHUNK)
    value_t = jnp.transpose(value_ref[...].astype(F32)).astype(BF16)
    gate_t = jnp.transpose(gate_ref[...].astype(F32) * 0.5).astype(BF16)
    return gain, bias, jnp.concatenate([value_t, gate_t], axis=0)


def project_chunk(params, pair_ref, mask_ref, out_ref, mixed, start):
    gain, bias, weight = params
    for row in range(SUB):
        turned = jnp.transpose(pair_ref[row, start : start + CHUNK, :]).astype(F32)
        half_mask = mask_ref[row : row + 1, start : start + CHUNK].astype(F32) * 0.5
        centred = turned - jnp.sum(turned, axis=0, keepdims=True) * (1.0 / 128)
        variance = jnp.sum(centred * centred, axis=0, keepdims=True) * (1.0 / 128)
        normed = (centred * lax.rsqrt(variance + EPS) * gain + bias).astype(BF16)
        both = dot(weight, normed, ((1,), (0,)))
        half = both[:128] * half_mask
        first = (start // CHUNK * SUB + row) * STRIDE
        mixed[first : first + 128, :] = half + half * jnp.tanh(both[128:])
    for part in range(PARTS):
        first = start // CHUNK * SUB * STRIDE + part * OWN
        pieces = [mixed[pl.ds(first + k, SUB, stride=STRIDE), :] for k in range(OWN)]
        out_ref[part, :, start : start + CHUNK] = jnp.concatenate(pieces, axis=0).astype(BF16)


def project_kernel(side_ref, pair_ref, mask_ref, gain_ref, bias_ref, value_ref, gate_ref, out_ref, mixed):
    params = projection(gain_ref, bias_ref, value_ref, gate_ref)
    for start in range(0, pair_ref.shape[1], CHUNK):
        project_chunk(params, pair_ref, mask_ref, out_ref, mixed, start)


def project(pair, mask, gain, bias, w_value, w_gate, side, limit):
    length = pair.shape[1]
    width = 512
    tokens = SUB * length
    whole = lambda i, side: (0, 0)
    column = lambda i, side: (0, side[0])
    spec = pltpu.PrefetchScalarGridSpec(
        num_scalar_prefetch=1,
        grid=(length // width,),
        in_specs=[
            pl.BlockSpec((SUB, width, 128), lambda i, side: (0, i, 0)),
            pl.BlockSpec((SUB, width), lambda i, side: (0, i)),
            pl.BlockSpec((1, 128), whole),
            pl.BlockSpec((1, 128), whole),
            pl.BlockSpec((128, 128), column),
            pl.BlockSpec((128, 128), column),
        ],
        out_specs=pl.BlockSpec((PARTS, OWN * SUB, width), lambda i, side: (0, 0, i)),
        scratch_shapes=[pltpu.VMEM((SUB * STRIDE * (width // CHUNK) + 136, 128), F32)],
    )
    return pl.pallas_call(
        project_kernel,
        grid_spec=spec,
        out_shape=jax.ShapeDtypeStruct((PARTS, OWN * SUB, length), BF16),
        compiler_params=pltpu.CompilerParams(vmem_limit_bytes=limit),
        cost_estimate=pl.CostEstimate(
            flops=tokens * 128 * 384 * 2, bytes_accessed=tokens * 512, transcendentals=tokens * 128
        ),
        name="project",
    )(side.reshape(1), pair, mask, gain, bias, w_value, w_gate)


def rows_of(ref, parts, tokens, half):
    both = ref[parts, half * 16 : (half + 1) * 16, tokens].astype(F32)
    count, _, width = both.shape
    return [
        both[:, k * SUB : (k + 1) * SUB, :].reshape(count * SUB, width).astype(BF16)
        for k in range(2)
    ]


def corner_kernel(left_ref, right_ref, out_ref):
    every = slice(None)
    for half in range(OWN // 2):
        left = rows_of(left_ref, every, every, half)
        right = rows_of(right_ref, every, every, half)
        for k in range(2):
            product = dot(left[k], right[k], ((1,), (1,)))
            out_ref[half * 2 + k] = jnp.concatenate(
                [product[: BLOCK // 2], product[BLOCK // 2 :]], axis=1
            ).astype(BF16)


def corner(left, early):
    shape = left.shape
    return pl.pallas_call(
        corner_kernel,
        grid=(1,),
        in_specs=[
            pl.BlockSpec(shape, lambda i: (0, 0, 0)),
            pl.BlockSpec(shape, lambda i: (STEPS - 2, 0, 0)),
        ],
        out_specs=pl.BlockSpec((OWN, BLOCK // 2, 2 * BLOCK), lambda i: (0, 0, 0)),
        out_shape=jax.ShapeDtypeStruct((OWN, BLOCK // 2, 2 * BLOCK), BF16),
        compiler_params=pltpu.CompilerParams(vmem_limit_bytes=VMEM_SMALL),
        cost_estimate=pl.CostEstimate(
            flops=2 * 4 * 64 * 64 * 2048, bytes_accessed=2 * 1024 * 1024, transcendentals=0
        ),
        name="corner",
    )(left, early)


def contract_kernel(
    early_hbm, late_hbm, after_hbm, corner_hbm, out_ref, early, late, after, corner_ref, total, sems, corner_sem
):
    halves = OWN // 2
    pairs = ((early_hbm, early), (late_hbm, late), (after_hbm, after))
    copies = {}
    for k, tokens in enumerate(DOTS):
        for half in range(halves):
            rows = pl.ds(half * 16, 16)
            copies[k, half] = [
                pltpu.make_async_copy(
                    source.at[:, rows, pl.ds(*tokens)],
                    target.at[:, rows, pl.ds(*tokens)],
                    sems.at[k * halves + half, j],
                )
                for j, (source, target) in enumerate(pairs)
            ]
            for copy in copies[k, half]:
                copy.start()
    corner_copy = pltpu.make_async_copy(corner_hbm, corner_ref, corner_sem)
    corner_copy.start()
    groups = BLOCK // SUB
    rest = slice(0, (STEPS - 1) * groups)
    last = slice((STEPS - 1) * groups, STEPS * groups)
    for k, (begin, length) in enumerate(DOTS):
        tokens = slice(begin, begin + length)
        for half in range(halves):
            for copy in copies[k, half]:
                copy.wait()
            early_rest, early_last = (rows_of(early, p, tokens, half) for p in (rest, last))
            late_rest, late_last = (rows_of(late, p, tokens, half) for p in (rest, last))
            following = rows_of(after, slice(None), tokens, half)
            for j in range(2):
                left = jnp.concatenate([late_rest[j], early_last[j]], axis=0)
                window = jnp.concatenate([early_rest[j], late_last[j], following[j]], axis=0)
                channel = half * 2 + j
                near = dot(left, window[: STEPS * BLOCK], ((1,), (1,)))
                far = dot(left[BLOCK:], window[STEPS * BLOCK :], ((1,), (1,)))
                for part, rows, columns_ in (
                    (near, slice(0, None), slice(0, STEPS * BLOCK)),
                    (far, slice(BLOCK, None), slice(STEPS * BLOCK, None)),
                ):
                    if k == 0:
                        total[channel, rows, columns_] = part
                    else:
                        total[channel, rows, columns_] += part
            if k < len(DOTS) - 1:
                continue
            if half == 0:
                corner_copy.wait()
            for block in range(STEPS):
                band = []
                for channel in (half * 2, half * 2 + 1):
                    rows = total[
                        channel, block * BLOCK : (block + 1) * BLOCK, block * BLOCK : (block + STEPS) * BLOCK
                    ]
                    if block == STEPS - 1:
                        folded = corner_ref[channel].astype(F32)
                        final = jnp.concatenate([folded[:, :BLOCK], folded[:, BLOCK:]], axis=0)
                        rows = jnp.concatenate([rows, final], axis=1)
                    band.append(rows.reshape(groups, SUB, STEPS * BLOCK))
                out_ref[
                    block * groups : (block + 1) * groups, half * 16 : (half + 1) * 16, :
                ] = jnp.concatenate(band, axis=1).astype(BF16)


def contract(early, late, after, returned):
    hbm = pl.BlockSpec(memory_space=pltpu.HBM)
    anywhere = pl.BlockSpec(memory_space=pl.ANY)
    vmem = pl.BlockSpec(memory_space=pltpu.VMEM)
    window = BLOCK * (2 * STEPS - 2)
    return pl.pallas_call(
        contract_kernel,
        in_specs=[hbm, hbm, anywhere, anywhere],
        out_specs=vmem,
        out_shape=jax.ShapeDtypeStruct((PARTS, OWN * SUB, STEPS * BLOCK), BF16),
        scratch_shapes=[pltpu.VMEM(v.shape, BF16) for v in (early, late, after)]
        + [
            pltpu.VMEM(returned.shape, BF16),
            pltpu.VMEM((OWN, BLOCK * STEPS, window), F32),
            pltpu.SemaphoreType.DMA((OWN // 2 * len(DOTS), 3)),
            pltpu.SemaphoreType.DMA(()),
        ],
        compiler_params=pltpu.CompilerParams(vmem_limit_bytes=VMEM_CONTRACT),
        cost_estimate=pl.CostEstimate(
            flops=2 * 4 * 256 * window * 2048, bytes_accessed=11 * 2**20, transcendentals=0
        ),
        name="contract",
    )(early, late, after, returned)


def finish_kernel(triangle_ref, gate_ref, gain_ref, bias_ref, w_ref, out_ref, scaled):
    width = triangle_ref.shape[2]
    values = triangle_ref[...].astype(F32).reshape(128, SUB, width)
    centred = values - jnp.sum(values, axis=0, keepdims=True) * (1.0 / 128)
    variance = jnp.sum(centred * centred, axis=0, keepdims=True) * (1.0 / 128)
    even = (centred * lax.rsqrt(variance + EPS)).reshape(128 * SUB, width)
    tiles = width // 128
    for tile in range(tiles):
        scaled[tile * SUB * 128 : (tile + 1) * SUB * 128, :] = even[:, tile * 128 : (tile + 1) * 128]
    gain = across(columns(gain_ref[...]), width)
    bias = across(columns(bias_ref[...]), width)
    for row in range(SUB):
        mine = [scaled[pl.ds(tile * SUB * 128 + row, 128, stride=SUB), :] for tile in range(tiles)]
        held = (jnp.concatenate(mine, axis=1) * gain + bias).astype(BF16)
        projected = dot(held, w_ref[...], ((0,), (0,)))
        out_ref[row] = (projected * gate_ref[row]).astype(BF16)


def finish(triangle, gate, gain, bias, w_out):
    width = 256
    whole = lambda i: (0, 0)
    return pl.pallas_call(
        finish_kernel,
        grid=(STEPS * BLOCK // width,),
        in_specs=[
            pl.BlockSpec((PARTS, OWN * SUB, width), lambda i: (0, 0, i)),
            pl.BlockSpec((SUB, width, 128), lambda i: (0, i, 0)),
            pl.BlockSpec((1, 128), whole),
            pl.BlockSpec((1, 128), whole),
            pl.BlockSpec((128, 128), whole),
        ],
        out_specs=pl.BlockSpec((SUB, width, 128), lambda i: (0, i, 0)),
        out_shape=jax.ShapeDtypeStruct((SUB, STEPS * BLOCK, 128), BF16),
        scratch_shapes=[pltpu.VMEM((SUB * width + SUB, 128), F32)],
        compiler_params=pltpu.CompilerParams(vmem_limit_bytes=VMEM_SMALL),
        cost_estimate=pl.CostEstimate(
            flops=SUB * 256 * 128 * 256, bytes_accessed=2 * 1024 * 1024, transcendentals=2048
        ),
        name="finish",
    )(triangle, gate, gain, bias, w_out)


def gate_kernel(block_ref, p0, p1, p2, p3, gain_ref, bias_ref, w_ref, out_ref):
    for k, ref in enumerate((p0, p1, p2, p3)):
        rows = ref[...].reshape(SUB * BLOCK, 128).astype(F32)
        centred = rows - jnp.sum(rows, axis=1, keepdims=True) * (1.0 / 128)
        variance = jnp.sum(centred * centred, axis=1, keepdims=True) * (1.0 / 128)
        normed = centred * lax.rsqrt(variance + EPS) * gain_ref[...] + bias_ref[...]
        half = dot(normed.astype(BF16), w_ref[...], ((1,), (0,))) * 0.5
        out_ref[:, k * BLOCK : (k + 1) * BLOCK, :] = (jnp.tanh(half) * 0.5 + 0.5).reshape(
            SUB, BLOCK, 128
        )


def output_gate(pair, gain, bias, out_gate_w, block):
    blocks = pair.shape[1] // BLOCK
    whole = lambda i, first: (0, 0)
    spec = pltpu.PrefetchScalarGridSpec(
        num_scalar_prefetch=1,
        grid=(1,),
        in_specs=[
            pl.BlockSpec(
                (SUB, BLOCK, 128), lambda i, first, k=k: (0, lax.rem(first[0] + k, blocks), 0)
            )
            for k in range(STEPS)
        ]
        + [
            pl.BlockSpec((1, 128), whole),
            pl.BlockSpec((1, 128), whole),
            pl.BlockSpec((128, 128), whole),
        ],
        out_specs=pl.BlockSpec((SUB, STEPS * BLOCK, 128), lambda i, first: (0, 0, 0)),
    )
    return pl.pallas_call(
        gate_kernel,
        grid_spec=spec,
        out_shape=jax.ShapeDtypeStruct((SUB, STEPS * BLOCK, 128), F32),
        compiler_params=pltpu.CompilerParams(vmem_limit_bytes=VMEM_SMALL),
        cost_estimate=pl.CostEstimate(
            flops=SUB * 256 * 128 * 256, bytes_accessed=2 * 1024 * 1024, transcendentals=2**18
        ),
        name="gate",
    )(block.astype(jnp.int32).reshape(1), pair, pair, pair, pair, gain, bias, out_gate_w)


def on_device(
    pair, pair_mask, in_gain, in_bias, w_value, w_gate, out_gate_w, out_gain, out_bias, w_out
):
    gain, bias = in_gain.reshape(1, 128), in_bias.reshape(1, 128)
    planes = lax.axis_size("z")
    down = [(i, (i - 1) % planes) for i in range(planes)]
    up = [(i, (i + 1) % planes) for i in range(planes)]
    place = lax.axis_index("yhi") * 2 + lax.axis_index("core")
    block = lax.axis_index("z") * STEPS + place
    groups = BLOCK // SUB

    def operand(side, limit):
        return project(pair, pair_mask, gain, bias, w_value, w_gate, side, limit)

    def spread(value):
        return lax.all_to_all(value, PLANE, 0, 0, tiled=True)

    side = jnp.where(place == STEPS - 1, 0, 1).astype(jnp.int32)
    early = spread(operand(side, VMEM_LIMIT))
    above = lax.ppermute(early[(STEPS - 1) * groups :], "z", up)
    after = lax.ppermute(early[: 2 * groups], "z", down)
    returned = lax.ppermute(corner(above, early), "z", down)
    late = spread(operand(1 - side, VMEM_SMALL))
    band = contract(early, late, after, returned)
    band, block = lax.optimization_barrier((band, block))
    gate = output_gate(pair, gain, bias, out_gate_w, block)
    triangle = spread(band)
    return finish(triangle, gate, out_gain.reshape(1, 128), out_bias.reshape(1, 128), w_out)


def solution(mesh):
    fine = Mesh(mesh.devices.reshape(4, 2, 8, 2, 2), ("x", "ylo", "z", "yhi", "core"))
    rows = ("z", "yhi", "core", "x", "ylo")
    placed = (P(rows, None, None), P(rows, None)) + (P(),) * 8
    return jax.shard_map(
        on_device,
        mesh=fine,
        in_specs=placed,
        out_specs=P(rows, None, None),
        check_vma=False,
    )
```

```python
import functools

import jax
import jax.numpy as jnp
from jax import lax
from jax.experimental import pallas as pl
from jax.experimental.pallas import tpu as pltpu
from jax.sharding import Mesh, PartitionSpec as P

EPS = 1e-05
BLOCK = 64
STEPS = 4
SUB = 8
PLANE = ("yhi", "core", "x", "ylo")
PARTS = 32
OWN = 4
DOTS = ((0, 768), (768, 1280))
CHUNK = 128
STRIDE = 130
F32 = jnp.float32
BF16 = jnp.bfloat16
VMEM_LIMIT = 60 * 1024 * 1024
VMEM_SMALL = 24 * 1024 * 1024
VMEM_CONTRACT = 52 * 1024 * 1024


def dot(a, b, dims):
    return lax.dot_general(a, b, (dims, ((), ())), preferred_element_type=F32)


def columns(row):
    return jnp.transpose(jnp.broadcast_to(row, (128, 128)))


def across(block, width):
    return jnp.concatenate([block] * (width // 128), axis=1)


def projection(gain_ref, bias_ref, value_ref, gate_ref):
    gain = across(columns(gain_ref[...]), CHUNK)
    bias = across(columns(bias_ref[...]), CHUNK)
    value_t = jnp.transpose(value_ref[...].astype(F32)).astype(BF16)
    gate_t = jnp.transpose(gate_ref[...].astype(F32) * 0.5).astype(BF16)
    return gain, bias, jnp.concatenate([value_t, gate_t], axis=0)


def project_chunk(params, pair_ref, mask_ref, out_ref, mixed, start):
    gain, bias, weight = params
    for row in range(SUB):
        turned = jnp.transpose(pair_ref[row, start : start + CHUNK, :]).astype(F32)
        half_mask = mask_ref[row : row + 1, start : start + CHUNK].astype(F32) * 0.5
        centred = turned - jnp.sum(turned, axis=0, keepdims=True) * (1.0 / 128)
        variance = jnp.sum(centred * centred, axis=0, keepdims=True) * (1.0 / 128)
        normed = (centred * lax.rsqrt(variance + EPS) * gain + bias).astype(BF16)
        both = dot(weight, normed, ((1,), (0,)))
        half = both[:128] * half_mask
        first = (start // CHUNK * SUB + row) * STRIDE
        mixed[first : first + 128, :] = half + half * jnp.tanh(both[128:])
    for part in range(PARTS):
        first = start // CHUNK * SUB * STRIDE + part * OWN
        pieces = [mixed[pl.ds(first + k, SUB, stride=STRIDE), :] for k in range(OWN)]
        out_ref[part, :, start : start + CHUNK] = jnp.concatenate(pieces, axis=0).astype(BF16)


def project_kernel(side_ref, pair_ref, mask_ref, gain_ref, bias_ref, value_ref, gate_ref, out_ref, mixed):
    params = projection(gain_ref, bias_ref, value_ref, gate_ref)
    for start in range(0, pair_ref.shape[1], CHUNK):
        project_chunk(params, pair_ref, mask_ref, out_ref, mixed, start)


def project(pair, mask, gain, bias, w_value, w_gate, side, limit):
    length = pair.shape[1]
    width = 512
    tokens = SUB * length
    whole = lambda i, side: (0, 0)
    column = lambda i, side: (0, side[0])
    spec = pltpu.PrefetchScalarGridSpec(
        num_scalar_prefetch=1,
        grid=(length // width,),
        in_specs=[
            pl.BlockSpec((SUB, width, 128), lambda i, side: (0, i, 0)),
            pl.BlockSpec((SUB, width), lambda i, side: (0, i)),
            pl.BlockSpec((1, 128), whole),
            pl.BlockSpec((1, 128), whole),
            pl.BlockSpec((128, 128), column),
            pl.BlockSpec((128, 128), column),
        ],
        out_specs=pl.BlockSpec((PARTS, OWN * SUB, width), lambda i, side: (0, 0, i)),
        scratch_shapes=[pltpu.VMEM((SUB * STRIDE * (width // CHUNK) + 136, 128), F32)],
    )
    return pl.pallas_call(
        project_kernel,
        grid_spec=spec,
        out_shape=jax.ShapeDtypeStruct((PARTS, OWN * SUB, length), BF16),
        compiler_params=pltpu.CompilerParams(vmem_limit_bytes=limit),
        cost_estimate=pl.CostEstimate(
            flops=tokens * 128 * 384 * 2, bytes_accessed=tokens * 512, transcendentals=tokens * 128
        ),
        name="project",
    )(side.reshape(1), pair, mask, gain, bias, w_value, w_gate)


def rows_of(ref, parts, tokens, half):
    both = ref[parts, half * 16 : (half + 1) * 16, tokens].astype(F32)
    count, _, width = both.shape
    return [
        both[:, k * SUB : (k + 1) * SUB, :].reshape(count * SUB, width).astype(BF16)
        for k in range(2)
    ]


def corner_kernel(left_ref, right_ref, out_ref):
    every = slice(None)
    for half in range(OWN // 2):
        left = rows_of(left_ref, every, every, half)
        right = rows_of(right_ref, every, every, half)
        for k in range(2):
            product = dot(left[k], right[k], ((1,), (1,)))
            out_ref[half * 2 + k] = jnp.concatenate(
                [product[: BLOCK // 2], product[BLOCK // 2 :]], axis=1
            ).astype(BF16)


def corner(left, early):
    shape = left.shape
    return pl.pallas_call(
        corner_kernel,
        grid=(1,),
        in_specs=[
            pl.BlockSpec(shape, lambda i: (0, 0, 0)),
            pl.BlockSpec(shape, lambda i: (STEPS - 2, 0, 0)),
        ],
        out_specs=pl.BlockSpec((OWN, BLOCK // 2, 2 * BLOCK), lambda i: (0, 0, 0)),
        out_shape=jax.ShapeDtypeStruct((OWN, BLOCK // 2, 2 * BLOCK), BF16),
        compiler_params=pltpu.CompilerParams(vmem_limit_bytes=VMEM_SMALL),
        cost_estimate=pl.CostEstimate(
            flops=2 * 4 * 64 * 64 * 2048, bytes_accessed=2 * 1024 * 1024, transcendentals=0
        ),
        name="corner",
    )(left, early)


def contract_kernel(
    early_hbm, late_hbm, after_hbm, corner_hbm, out_hbm, early, late, after, corner_ref, out_ref, total, sems,
    corner_sem, out_sems
):
    halves = OWN // 2
    pairs = ((early_hbm, early), (late_hbm, late), (after_hbm, after))
    copies = {}
    for k, tokens in enumerate(DOTS):
        for half in range(halves):
            rows = pl.ds(half * 16, 16)
            copies[k, half] = [
                pltpu.make_async_copy(
                    source.at[:, rows, pl.ds(*tokens)],
                    target.at[:, rows, pl.ds(*tokens)],
                    sems.at[k * halves + half, j],
                )
                for j, (source, target) in enumerate(pairs)
            ]
            for copy in copies[k, half]:
                copy.start()
    corner_copy = pltpu.make_async_copy(corner_hbm, corner_ref, corner_sem)
    corner_copy.start()
    stores = [
        pltpu.make_async_copy(
            out_ref.at[:, pl.ds(half * 16, 16), :], out_hbm.at[:, pl.ds(half * 16, 16), :], out_sems.at[half]
        )
        for half in range(halves)
    ]
    groups = BLOCK // SUB
    rest = slice(0, (STEPS - 1) * groups)
    last = slice((STEPS - 1) * groups, STEPS * groups)
    for k, (begin, length) in enumerate(DOTS):
        tokens = slice(begin, begin + length)
        for half in range(halves):
            for copy in copies[k, half]:
                copy.wait()
            early_rest, early_last = (rows_of(early, p, tokens, half) for p in (rest, last))
            late_rest, late_last = (rows_of(late, p, tokens, half) for p in (rest, last))
            following = rows_of(after, slice(None), tokens, half)
            for j in range(2):
                left = jnp.concatenate([late_rest[j], early_last[j]], axis=0)
                window = jnp.concatenate([early_rest[j], late_last[j], following[j]], axis=0)
                channel = half * 2 + j
                near = dot(left, window[: STEPS * BLOCK], ((1,), (1,)))
                far = dot(left[BLOCK:], window[STEPS * BLOCK :], ((1,), (1,)))
                for part, rows, columns_ in (
                    (near, slice(0, None), slice(0, STEPS * BLOCK)),
                    (far, slice(BLOCK, None), slice(STEPS * BLOCK, None)),
                ):
                    if k == 0:
                        total[channel, rows, columns_] = part
                    else:
                        total[channel, rows, columns_] += part
            if k < len(DOTS) - 1:
                continue
            if half == 0:
                corner_copy.wait()
            for block in range(STEPS):
                band = []
                for channel in (half * 2, half * 2 + 1):
                    rows = total[
                        channel, block * BLOCK : (block + 1) * BLOCK, block * BLOCK : (block + STEPS) * BLOCK
                    ]
                    if block == STEPS - 1:
                        folded = corner_ref[channel].astype(F32)
                        final = jnp.concatenate([folded[:, :BLOCK], folded[:, BLOCK:]], axis=0)
                        rows = jnp.concatenate([rows, final], axis=1)
                    band.append(rows.reshape(groups, SUB, STEPS * BLOCK))
                out_ref[
                    block * groups : (block + 1) * groups, half * 16 : (half + 1) * 16, :
                ] = jnp.concatenate(band, axis=1).astype(BF16)
            stores[half].start()
    for store in stores:
        store.wait()


def contract(early, late, after, returned):
    hbm = pl.BlockSpec(memory_space=pltpu.HBM)
    anywhere = pl.BlockSpec(memory_space=pl.ANY)
    window = BLOCK * (2 * STEPS - 2)
    return pl.pallas_call(
        contract_kernel,
        in_specs=[hbm, hbm, anywhere, anywhere],
        out_specs=hbm,
        out_shape=jax.ShapeDtypeStruct((PARTS, OWN * SUB, STEPS * BLOCK), BF16),
        scratch_shapes=[pltpu.VMEM(v.shape, BF16) for v in (early, late, after)]
        + [
            pltpu.VMEM(returned.shape, BF16),
            pltpu.VMEM((PARTS, OWN * SUB, STEPS * BLOCK), BF16),
            pltpu.VMEM((OWN, BLOCK * STEPS, window), F32),
            pltpu.SemaphoreType.DMA((OWN // 2 * len(DOTS), 3)),
            pltpu.SemaphoreType.DMA(()),
            pltpu.SemaphoreType.DMA((OWN // 2,)),
        ],
        compiler_params=pltpu.CompilerParams(vmem_limit_bytes=VMEM_CONTRACT),
        cost_estimate=pl.CostEstimate(
            flops=2 * 4 * 256 * window * 2048, bytes_accessed=11 * 2**20, transcendentals=0
        ),
        name="contract",
    )(early, late, after, returned)


def finish_kernel(triangle_ref, gate_ref, gain_ref, bias_ref, w_ref, out_ref, scaled):
    width = triangle_ref.shape[2]
    values = triangle_ref[...].astype(F32).reshape(128, SUB, width)
    centred = values - jnp.sum(values, axis=0, keepdims=True) * (1.0 / 128)
    variance = jnp.sum(centred * centred, axis=0, keepdims=True) * (1.0 / 128)
    even = (centred * lax.rsqrt(variance + EPS)).reshape(128 * SUB, width)
    tiles = width // 128
    for tile in range(tiles):
        scaled[tile * SUB * 128 : (tile + 1) * SUB * 128, :] = even[:, tile * 128 : (tile + 1) * 128]
    gain = across(columns(gain_ref[...]), width)
    bias = across(columns(bias_ref[...]), width)
    for row in range(SUB):
        mine = [scaled[pl.ds(tile * SUB * 128 + row, 128, stride=SUB), :] for tile in range(tiles)]
        held = (jnp.concatenate(mine, axis=1) * gain + bias).astype(BF16)
        projected = dot(held, w_ref[...], ((0,), (0,)))
        out_ref[row] = (projected * gate_ref[row]).astype(BF16)


def finish(triangle, gate, gain, bias, w_out):
    width = 256
    whole = lambda i: (0, 0)
    return pl.pallas_call(
        finish_kernel,
        grid=(STEPS * BLOCK // width,),
        in_specs=[
            pl.BlockSpec((PARTS, OWN * SUB, width), lambda i: (0, 0, i)),
            pl.BlockSpec((SUB, width, 128), lambda i: (0, i, 0)),
            pl.BlockSpec((1, 128), whole),
            pl.BlockSpec((1, 128), whole),
            pl.BlockSpec((128, 128), whole),
        ],
        out_specs=pl.BlockSpec((SUB, width, 128), lambda i: (0, i, 0)),
        out_shape=jax.ShapeDtypeStruct((SUB, STEPS * BLOCK, 128), BF16),
        scratch_shapes=[pltpu.VMEM((SUB * width + SUB, 128), F32)],
        compiler_params=pltpu.CompilerParams(vmem_limit_bytes=VMEM_SMALL),
        cost_estimate=pl.CostEstimate(
            flops=SUB * 256 * 128 * 256, bytes_accessed=2 * 1024 * 1024, transcendentals=2048
        ),
        name="finish",
    )(triangle, gate, gain, bias, w_out)


def gate_kernel(block_ref, p0, p1, p2, p3, gain_ref, bias_ref, w_ref, out_ref):
    for k, ref in enumerate((p0, p1, p2, p3)):
        rows = ref[...].reshape(SUB * BLOCK, 128).astype(F32)
        centred = rows - jnp.sum(rows, axis=1, keepdims=True) * (1.0 / 128)
        variance = jnp.sum(centred * centred, axis=1, keepdims=True) * (1.0 / 128)
        normed = centred * lax.rsqrt(variance + EPS) * gain_ref[...] + bias_ref[...]
        half = dot(normed.astype(BF16), w_ref[...], ((1,), (0,))) * 0.5
        out_ref[:, k * BLOCK : (k + 1) * BLOCK, :] = (jnp.tanh(half) * 0.5 + 0.5).reshape(
            SUB, BLOCK, 128
        )


def output_gate(pair, gain, bias, out_gate_w, block):
    blocks = pair.shape[1] // BLOCK
    whole = lambda i, first: (0, 0)
    spec = pltpu.PrefetchScalarGridSpec(
        num_scalar_prefetch=1,
        grid=(1,),
        in_specs=[
            pl.BlockSpec(
                (SUB, BLOCK, 128), lambda i, first, k=k: (0, lax.rem(first[0] + k, blocks), 0)
            )
            for k in range(STEPS)
        ]
        + [
            pl.BlockSpec((1, 128), whole),
            pl.BlockSpec((1, 128), whole),
            pl.BlockSpec((128, 128), whole),
        ],
        out_specs=pl.BlockSpec((SUB, STEPS * BLOCK, 128), lambda i, first: (0, 0, 0)),
    )
    return pl.pallas_call(
        gate_kernel,
        grid_spec=spec,
        out_shape=jax.ShapeDtypeStruct((SUB, STEPS * BLOCK, 128), F32),
        compiler_params=pltpu.CompilerParams(vmem_limit_bytes=VMEM_SMALL),
        cost_estimate=pl.CostEstimate(
            flops=SUB * 256 * 128 * 256, bytes_accessed=2 * 1024 * 1024, transcendentals=2**18
        ),
        name="gate",
    )(block.astype(jnp.int32).reshape(1), pair, pair, pair, pair, gain, bias, out_gate_w)


def on_device(
    pair, pair_mask, in_gain, in_bias, w_value, w_gate, out_gate_w, out_gain, out_bias, w_out
):
    gain, bias = in_gain.reshape(1, 128), in_bias.reshape(1, 128)
    planes = lax.axis_size("z")
    down = [(i, (i - 1) % planes) for i in range(planes)]
    up = [(i, (i + 1) % planes) for i in range(planes)]
    place = lax.axis_index("yhi") * 2 + lax.axis_index("core")
    block = lax.axis_index("z") * STEPS + place
    groups = BLOCK // SUB

    def operand(side, limit):
        return project(pair, pair_mask, gain, bias, w_value, w_gate, side, limit)

    def spread(value):
        return lax.all_to_all(value, PLANE, 0, 0, tiled=True)

    side = jnp.where(place == STEPS - 1, 0, 1).astype(jnp.int32)
    early = spread(operand(side, VMEM_LIMIT))
    above = lax.ppermute(early[(STEPS - 1) * groups :], "z", up)
    after = lax.ppermute(early[: 2 * groups], "z", down)
    returned = lax.ppermute(corner(above, early), "z", down)
    late = spread(operand(1 - side, VMEM_SMALL))
    band = contract(early, late, after, returned)
    band, block = lax.optimization_barrier((band, block))
    gate = output_gate(pair, gain, bias, out_gate_w, block)
    triangle = spread(band)
    return finish(triangle, gate, out_gain.reshape(1, 128), out_bias.reshape(1, 128), w_out)


def solution(mesh):
    fine = Mesh(mesh.devices.reshape(4, 2, 8, 2, 2), ("x", "ylo", "z", "yhi", "core"))
    rows = ("z", "yhi", "core", "x", "ylo")
    placed = (P(rows, None, None), P(rows, None)) + (P(),) * 8
    return jax.shard_map(
        on_device,
        mesh=fine,
        in_specs=placed,
        out_specs=P(rows, None, None),
        check_vma=False,
    )
```

```python
import functools

import jax
import jax.numpy as jnp
from jax import lax
from jax.experimental import pallas as pl
from jax.experimental.pallas import tpu as pltpu
from jax.sharding import Mesh, PartitionSpec as P

EPS = 1e-05
BLOCK = 64
STEPS = 4
SUB = 8
PLANE = ("yhi", "core", "x", "ylo")
PARTS = 32
OWN = 4
DOTS = ((0, 768), (768, 1280))
CHUNK = 128
STRIDE = 130
F32 = jnp.float32
BF16 = jnp.bfloat16
VMEM_LIMIT = 60 * 1024 * 1024
VMEM_SMALL = 24 * 1024 * 1024
VMEM_CONTRACT = 52 * 1024 * 1024


def dot(a, b, dims):
    return lax.dot_general(a, b, (dims, ((), ())), preferred_element_type=F32)


def columns(row):
    return jnp.transpose(jnp.broadcast_to(row, (128, 128)))


def across(block, width):
    return jnp.concatenate([block] * (width // 128), axis=1)


def projection(gain_ref, bias_ref, value_ref, gate_ref):
    gain = across(columns(gain_ref[...]), CHUNK)
    bias = across(columns(bias_ref[...]), CHUNK)
    value_t = jnp.transpose(value_ref[...].astype(F32)).astype(BF16)
    gate_t = jnp.transpose(gate_ref[...].astype(F32) * 0.5).astype(BF16)
    return gain, bias, jnp.concatenate([value_t, gate_t], axis=0)


def project_chunk(params, pair_ref, mask_ref, out_ref, mixed, start):
    gain, bias, weight = params
    for row in range(SUB):
        turned = jnp.transpose(pair_ref[row, start : start + CHUNK, :]).astype(F32)
        half_mask = mask_ref[row : row + 1, start : start + CHUNK].astype(F32) * 0.5
        centred = turned - jnp.sum(turned, axis=0, keepdims=True) * (1.0 / 128)
        variance = jnp.sum(centred * centred, axis=0, keepdims=True) * (1.0 / 128)
        normed = (centred * lax.rsqrt(variance + EPS) * gain + bias).astype(BF16)
        both = dot(weight, normed, ((1,), (0,)))
        half = both[:128] * half_mask
        first = (start // CHUNK * SUB + row) * STRIDE
        mixed[first : first + 128, :] = half + half * jnp.tanh(both[128:])
    for part in range(PARTS):
        first = start // CHUNK * SUB * STRIDE + part * OWN
        pieces = [mixed[pl.ds(first + k, SUB, stride=STRIDE), :] for k in range(OWN)]
        out_ref[part, :, start : start + CHUNK] = jnp.concatenate(pieces, axis=0).astype(BF16)


def project_kernel(side_ref, pair_ref, mask_ref, gain_ref, bias_ref, value_ref, gate_ref, out_ref, mixed):
    params = projection(gain_ref, bias_ref, value_ref, gate_ref)
    for start in range(0, pair_ref.shape[1], CHUNK):
        project_chunk(params, pair_ref, mask_ref, out_ref, mixed, start)


def project(pair, mask, gain, bias, w_value, w_gate, side, limit):
    length = pair.shape[1]
    width = 512
    tokens = SUB * length
    whole = lambda i, side: (0, 0)
    column = lambda i, side: (0, side[0])
    spec = pltpu.PrefetchScalarGridSpec(
        num_scalar_prefetch=1,
        grid=(length // width,),
        in_specs=[
            pl.BlockSpec((SUB, width, 128), lambda i, side: (0, i, 0)),
            pl.BlockSpec((SUB, width), lambda i, side: (0, i)),
            pl.BlockSpec((1, 128), whole),
            pl.BlockSpec((1, 128), whole),
            pl.BlockSpec((128, 128), column),
            pl.BlockSpec((128, 128), column),
        ],
        out_specs=pl.BlockSpec((PARTS, OWN * SUB, width), lambda i, side: (0, 0, i)),
        scratch_shapes=[pltpu.VMEM((SUB * STRIDE * (width // CHUNK) + 136, 128), F32)],
    )
    return pl.pallas_call(
        project_kernel,
        grid_spec=spec,
        out_shape=jax.ShapeDtypeStruct((PARTS, OWN * SUB, length), BF16),
        compiler_params=pltpu.CompilerParams(vmem_limit_bytes=limit),
        cost_estimate=pl.CostEstimate(
            flops=tokens * 128 * 384 * 2, bytes_accessed=tokens * 512, transcendentals=tokens * 128
        ),
        name="project",
    )(side.reshape(1), pair, mask, gain, bias, w_value, w_gate)


def rows_of(ref, parts, tokens, half):
    both = ref[parts, half * 16 : (half + 1) * 16, tokens].astype(F32)
    count, _, width = both.shape
    return [
        both[:, k * SUB : (k + 1) * SUB, :].reshape(count * SUB, width).astype(BF16)
        for k in range(2)
    ]


def corner_kernel(left_ref, right_ref, out_ref):
    every = slice(None)
    for half in range(OWN // 2):
        left = rows_of(left_ref, every, every, half)
        right = rows_of(right_ref, every, every, half)
        for k in range(2):
            product = dot(left[k], right[k], ((1,), (1,)))
            out_ref[half * 2 + k] = jnp.concatenate(
                [product[: BLOCK // 2], product[BLOCK // 2 :]], axis=1
            ).astype(BF16)


def corner(left, early):
    shape = left.shape
    return pl.pallas_call(
        corner_kernel,
        grid=(1,),
        in_specs=[
            pl.BlockSpec(shape, lambda i: (0, 0, 0)),
            pl.BlockSpec(shape, lambda i: (STEPS - 2, 0, 0)),
        ],
        out_specs=pl.BlockSpec((OWN, BLOCK // 2, 2 * BLOCK), lambda i: (0, 0, 0)),
        out_shape=jax.ShapeDtypeStruct((OWN, BLOCK // 2, 2 * BLOCK), BF16),
        compiler_params=pltpu.CompilerParams(vmem_limit_bytes=VMEM_SMALL),
        cost_estimate=pl.CostEstimate(
            flops=2 * 4 * 64 * 64 * 2048, bytes_accessed=2 * 1024 * 1024, transcendentals=0
        ),
        name="corner",
    )(left, early)


def contract_kernel(
    early_hbm, late_hbm, after_hbm, corner_hbm, out_hbm, early, late, after, corner_ref, out_ref, total, sems,
    corner_sem, out_sems
):
    halves = OWN // 2
    pairs = ((early_hbm, early), (late_hbm, late), (after_hbm, after))
    copies = {}
    for k, tokens in enumerate(DOTS):
        for half in range(halves):
            rows = pl.ds(half * 16, 16)
            copies[k, half] = [
                pltpu.make_async_copy(
                    source.at[:, rows, pl.ds(*tokens)],
                    target.at[:, rows, pl.ds(*tokens)],
                    sems.at[k * halves + half, j],
                )
                for j, (source, target) in enumerate(pairs)
            ]
            for copy in copies[k, half]:
                copy.start()
    corner_copy = pltpu.make_async_copy(corner_hbm, corner_ref, corner_sem)
    corner_copy.start()
    stores = [
        pltpu.make_async_copy(
            out_ref.at[:, pl.ds(half * 16, 16), :], out_hbm.at[:, pl.ds(half * 16, 16), :], out_sems.at[half]
        )
        for half in range(halves)
    ]
    groups = BLOCK // SUB
    rest = slice(0, (STEPS - 1) * groups)
    last = slice((STEPS - 1) * groups, STEPS * groups)
    for k, (begin, length) in enumerate(DOTS):
        tokens = slice(begin, begin + length)
        for half in range(halves):
            for copy in copies[k, half]:
                copy.wait()
            early_rest, early_last = (rows_of(early, p, tokens, half) for p in (rest, last))
            late_rest, late_last = (rows_of(late, p, tokens, half) for p in (rest, last))
            following = rows_of(after, slice(None), tokens, half)
            for j in range(2):
                left = jnp.concatenate([late_rest[j], early_last[j]], axis=0)
                window = jnp.concatenate([early_rest[j], late_last[j], following[j]], axis=0)
                channel = half * 2 + j
                near = dot(left, window[: STEPS * BLOCK], ((1,), (1,)))
                far = dot(left[BLOCK:], window[STEPS * BLOCK :], ((1,), (1,)))
                for part, rows, columns_ in (
                    (near, slice(0, None), slice(0, STEPS * BLOCK)),
                    (far, slice(BLOCK, None), slice(STEPS * BLOCK, None)),
                ):
                    if k == 0:
                        total[channel, rows, columns_] = part
                    else:
                        total[channel, rows, columns_] += part
            if k < len(DOTS) - 1:
                continue
            if half == 0:
                corner_copy.wait()
            for block in range(STEPS):
                band = []
                for channel in (half * 2, half * 2 + 1):
                    rows = total[
                        channel, block * BLOCK : (block + 1) * BLOCK, block * BLOCK : (block + STEPS) * BLOCK
                    ]
                    if block == STEPS - 1:
                        folded = corner_ref[channel].astype(F32)
                        final = jnp.concatenate([folded[:, :BLOCK], folded[:, BLOCK:]], axis=0)
                        rows = jnp.concatenate([rows, final], axis=1)
                    band.append(rows.reshape(groups, SUB, STEPS * BLOCK))
                out_ref[
                    block * groups : (block + 1) * groups, half * 16 : (half + 1) * 16, :
                ] = jnp.concatenate(band, axis=1).astype(BF16)
            stores[half].start()
    for store in stores:
        store.wait()


def contract(early, late, after, returned):
    hbm = pl.BlockSpec(memory_space=pltpu.HBM)
    anywhere = pl.BlockSpec(memory_space=pl.ANY)
    window = BLOCK * (2 * STEPS - 2)
    return pl.pallas_call(
        contract_kernel,
        in_specs=[hbm, hbm, anywhere, anywhere],
        out_specs=hbm,
        out_shape=jax.ShapeDtypeStruct((PARTS, OWN * SUB, STEPS * BLOCK), BF16),
        scratch_shapes=[pltpu.VMEM(v.shape, BF16) for v in (early, late, after)]
        + [
            pltpu.VMEM(returned.shape, BF16),
            pltpu.VMEM((PARTS, OWN * SUB, STEPS * BLOCK), BF16),
            pltpu.VMEM((OWN, BLOCK * STEPS, window), F32),
            pltpu.SemaphoreType.DMA((OWN // 2 * len(DOTS), 3)),
            pltpu.SemaphoreType.DMA(()),
            pltpu.SemaphoreType.DMA((OWN // 2,)),
        ],
        compiler_params=pltpu.CompilerParams(vmem_limit_bytes=VMEM_CONTRACT),
        cost_estimate=pl.CostEstimate(
            flops=2 * 4 * 256 * window * 2048, bytes_accessed=11 * 2**20, transcendentals=0
        ),
        name="contract",
    )(early, late, after, returned)


def finish_kernel(triangle_ref, gate_ref, gain_ref, bias_ref, w_ref, out_hbm, scaled, out_ref, sems):
    width = triangle_ref.shape[2]
    values = triangle_ref[...].astype(F32).reshape(128, SUB, width)
    centred = values - jnp.sum(values, axis=0, keepdims=True) * (1.0 / 128)
    variance = jnp.sum(centred * centred, axis=0, keepdims=True) * (1.0 / 128)
    even = (centred * lax.rsqrt(variance + EPS)).reshape(128 * SUB, width)
    tiles = width // 128
    for tile in range(tiles):
        scaled[tile * SUB * 128 : (tile + 1) * SUB * 128, :] = even[:, tile * 128 : (tile + 1) * 128]
    gain = across(columns(gain_ref[...]), width)
    bias = across(columns(bias_ref[...]), width)
    for row in range(SUB):
        mine = [scaled[pl.ds(tile * SUB * 128 + row, 128, stride=SUB), :] for tile in range(tiles)]
        held = (jnp.concatenate(mine, axis=1) * gain + bias).astype(BF16)
        projected = dot(held, w_ref[...], ((0,), (0,)))
        out_ref[row] = (projected * gate_ref[row]).astype(BF16)
        pltpu.make_async_copy(out_ref.at[row], out_hbm.at[row], sems.at[row]).start()
    for row in range(SUB):
        pltpu.make_async_copy(out_ref.at[row], out_hbm.at[row], sems.at[row]).wait()


def finish(triangle, gate, gain, bias, w_out):
    width = 256
    whole = lambda i: (0, 0)
    return pl.pallas_call(
        finish_kernel,
        grid=(STEPS * BLOCK // width,),
        in_specs=[
            pl.BlockSpec((PARTS, OWN * SUB, width), lambda i: (0, 0, i)),
            pl.BlockSpec((SUB, width, 128), lambda i: (0, i, 0)),
            pl.BlockSpec((1, 128), whole),
            pl.BlockSpec((1, 128), whole),
            pl.BlockSpec((128, 128), whole),
        ],
        out_specs=pl.BlockSpec(memory_space=pltpu.HBM),
        out_shape=jax.ShapeDtypeStruct((SUB, STEPS * BLOCK, 128), BF16),
        scratch_shapes=[
            pltpu.VMEM((SUB * width + SUB, 128), F32),
            pltpu.VMEM((SUB, width, 128), BF16),
            pltpu.SemaphoreType.DMA((SUB,)),
        ],
        compiler_params=pltpu.CompilerParams(vmem_limit_bytes=VMEM_SMALL),
        cost_estimate=pl.CostEstimate(
            flops=SUB * 256 * 128 * 256, bytes_accessed=2 * 1024 * 1024, transcendentals=2048
        ),
        name="finish",
    )(triangle, gate, gain, bias, w_out)


def gate_kernel(block_ref, p0, p1, p2, p3, gain_ref, bias_ref, w_ref, out_ref):
    for k, ref in enumerate((p0, p1, p2, p3)):
        rows = ref[...].reshape(SUB * BLOCK, 128).astype(F32)
        centred = rows - jnp.sum(rows, axis=1, keepdims=True) * (1.0 / 128)
        variance = jnp.sum(centred * centred, axis=1, keepdims=True) * (1.0 / 128)
        normed = centred * lax.rsqrt(variance + EPS) * gain_ref[...] + bias_ref[...]
        half = dot(normed.astype(BF16), w_ref[...], ((1,), (0,))) * 0.5
        out_ref[:, k * BLOCK : (k + 1) * BLOCK, :] = (jnp.tanh(half) * 0.5 + 0.5).reshape(
            SUB, BLOCK, 128
        )


def output_gate(pair, gain, bias, out_gate_w, block):
    blocks = pair.shape[1] // BLOCK
    whole = lambda i, first: (0, 0)
    spec = pltpu.PrefetchScalarGridSpec(
        num_scalar_prefetch=1,
        grid=(1,),
        in_specs=[
            pl.BlockSpec(
                (SUB, BLOCK, 128), lambda i, first, k=k: (0, lax.rem(first[0] + k, blocks), 0)
            )
            for k in range(STEPS)
        ]
        + [
            pl.BlockSpec((1, 128), whole),
            pl.BlockSpec((1, 128), whole),
            pl.BlockSpec((128, 128), whole),
        ],
        out_specs=pl.BlockSpec((SUB, STEPS * BLOCK, 128), lambda i, first: (0, 0, 0)),
    )
    return pl.pallas_call(
        gate_kernel,
        grid_spec=spec,
        out_shape=jax.ShapeDtypeStruct((SUB, STEPS * BLOCK, 128), F32),
        compiler_params=pltpu.CompilerParams(vmem_limit_bytes=VMEM_SMALL),
        cost_estimate=pl.CostEstimate(
            flops=SUB * 256 * 128 * 256, bytes_accessed=2 * 1024 * 1024, transcendentals=2**18
        ),
        name="gate",
    )(block.astype(jnp.int32).reshape(1), pair, pair, pair, pair, gain, bias, out_gate_w)


def on_device(
    pair, pair_mask, in_gain, in_bias, w_value, w_gate, out_gate_w, out_gain, out_bias, w_out
):
    gain, bias = in_gain.reshape(1, 128), in_bias.reshape(1, 128)
    planes = lax.axis_size("z")
    down = [(i, (i - 1) % planes) for i in range(planes)]
    up = [(i, (i + 1) % planes) for i in range(planes)]
    place = lax.axis_index("yhi") * 2 + lax.axis_index("core")
    block = lax.axis_index("z") * STEPS + place
    groups = BLOCK // SUB

    def operand(side, limit):
        return project(pair, pair_mask, gain, bias, w_value, w_gate, side, limit)

    def spread(value):
        return lax.all_to_all(value, PLANE, 0, 0, tiled=True)

    side = jnp.where(place == STEPS - 1, 0, 1).astype(jnp.int32)
    early = spread(operand(side, VMEM_LIMIT))
    above = lax.ppermute(early[(STEPS - 1) * groups :], "z", up)
    after = lax.ppermute(early[: 2 * groups], "z", down)
    returned = lax.ppermute(corner(above, early), "z", down)
    late = spread(operand(1 - side, VMEM_SMALL))
    band = contract(early, late, after, returned)
    band, block = lax.optimization_barrier((band, block))
    gate = output_gate(pair, gain, bias, out_gate_w, block)
    triangle = spread(band)
    return finish(triangle, gate, out_gain.reshape(1, 128), out_bias.reshape(1, 128), w_out)


def solution(mesh):
    fine = Mesh(mesh.devices.reshape(4, 2, 8, 2, 2), ("x", "ylo", "z", "yhi", "core"))
    rows = ("z", "yhi", "core", "x", "ylo")
    placed = (P(rows, None, None), P(rows, None)) + (P(),) * 8
    return jax.shard_map(
        on_device,
        mesh=fine,
        in_specs=placed,
        out_specs=P(rows, None, None),
        check_vma=False,
    )
```
